256 devices in a mesh: img: 64 (over z, y, x_lo), txt: 4 (over x_hi, core).
Axes of the slice: x: 4 (x_hi: 2, x_lo: 2; x = x_hi * 2 + x_lo), y: 4, z: 8, core: 2. Of those that a mesh axis runs over, the one named last changes fastest.
Arguments:
- picture_vector_matrix: bfloat16 [65536, 1152], P(('img', 'txt')), may hold values from -1 to 1
- caption_vector_matrix: bfloat16 [65536, 1152], P(('img', 'txt')), may hold values from -1 to 1
- matched_caption_position: int32 [65536], P(('img', 'txt')), may hold values from 0 to 65535, as said below
- sharpness_factor: float32 [1], replicated, may hold values from 1 to 3
- pairwise_score_shift: float32 [1], replicated, may hold values from -3 to -1
Outputs:
- loss_rows: float32 [65536], P(('img', 'txt'))
- grad_images: float32 [65536, 1152], P(('img', 'txt'))
- text_embedding_gradient: float32 [65536, 1152], P(('img', 'txt'))
The draws below stay inside these ranges and needn't reach their ends.
Inputs may be any that keep to these rules, and one draw needn't show every extreme that they name: `matched_caption_position`: image rows g*1024 to (g+1)*1024 - 1 are paired one to one with the text rows of the same range, for every group g.
All inputs are finite; a program needn't handle non-finite values.
Results may differ from the reference program's by a relative error of at most 0.002.
Values may be sent and summed in bfloat16 or wider, within the bound.
A program may use at most 128 MiB of HBM per device.

```python
import math
import jax
import jax.numpy as jnp
from jax import lax

D = 1152
STEPS = 4
GROUP = 1024
NROWS = 65536


def draw_matched_caption_position(key, part):
    key = jax.random.fold_in(key, 7)
    groups = NROWS // GROUP
    group_keys = jax.random.split(key, groups)

    def shuffle(single_random_key):
        return jax.random.permutation(single_random_key, GROUP).astype(jnp.int32)
    shuffled = jax.vmap(shuffle)(group_keys)
    starts = jnp.arange(groups, dtype=jnp.int32)[:, None] * GROUP
    return (shuffled + starts).reshape(NROWS)


def levels(stream_key, dims, cuts, low, largest):
    gain, own = 1.0, jax.random.fold_in(stream_key, 6)
    for axis_at, parts in cuts:
        steps = jnp.exp(jax.random.uniform(jax.random.fold_in(own, axis_at), (parts,), jnp.float32, low / len(cuts), largest / len(cuts)))
        gain = gain * jnp.repeat(steps, dims[axis_at] // parts).reshape([-1 if axis == axis_at else 1 for axis in range(len(dims))])
    return gain


def gaussian(own_key, shape, spread, most, pieces=(), held_as=jnp.bfloat16):
    result = jax.random.normal(own_key, shape, jnp.float32) * spread
    if len(pieces) > 0:
        result = levels(own_key, shape, pieces, -0.22, 0.18) * result
    return jnp.clip(result, min=-most, max=most).astype(held_as)


def setup_inputs(seed: int = 0) -> dict:
    keys = jax.random.split(jax.random.key(seed), 6)
    picture_vector_matrix = gaussian(keys[0], (NROWS, D), (D ** -0.25), 1.0, ((0, 256),))
    caption_vector_matrix = gaussian(keys[1], (NROWS, D), (D ** -0.25), 1.0, ((0, 256),))
    matched_caption_position = draw_matched_caption_position(jax.random.fold_in(keys[5], 71), 0)
    sharpness_factor = jnp.clip(jnp.exp(jax.random.uniform(keys[3], (1,), jnp.float32, math.log(1.0), math.log(3.0))), 1.0, 3.0)
    pairwise_score_shift = jnp.clip(jax.random.uniform(keys[4], (1,), jnp.float32, -3.0, -1.0), -3.0, -1.0)
    return dict(picture_vector_matrix=picture_vector_matrix, caption_vector_matrix=caption_vector_matrix, matched_caption_position=matched_caption_position, sharpness_factor=sharpness_factor, pairwise_score_shift=pairwise_score_shift)


def panel_summands(picture_entries, matched_entries, caption_tile, holder_group, score_multiplier, displacement):
    similarity_matrix = lax.dot_general(picture_entries, caption_tile, (((1,), (1,)), ((), ())), preferred_element_type=jnp.float32)
    pairwise_scores = score_multiplier * similarity_matrix + displacement
    columns = holder_group * GROUP + jnp.arange(GROUP, dtype=jnp.int32)
    labels = (matched_entries[:, None] == columns[None, :]).astype(jnp.float32)
    signed = 2.0 * labels - 1.0
    entry_objective = jnp.sum(jax.nn.softplus(-signed * pairwise_scores), axis=1)
    derivative = (jax.nn.sigmoid(pairwise_scores) - labels).astype(jnp.bfloat16)
    return entry_objective, derivative


def reference(picture_vector_matrix, caption_vector_matrix, matched_caption_position, sharpness_factor, pairwise_score_shift):
    score_multiplier = sharpness_factor[0]
    displacement = pairwise_score_shift[0]
    groups = NROWS // GROUP
    width = picture_vector_matrix.shape[1]

    def visit(caption_objective_aggregate, group_at):
        start = (group_at * GROUP).astype(jnp.int32)
        picture_entries = lax.dynamic_slice_in_dim(picture_vector_matrix, start, GROUP, 0)
        matched_entries = lax.dynamic_slice_in_dim(matched_caption_position, start, GROUP, 0)
        objective_aggregate = jnp.zeros((GROUP,), jnp.float32)
        picture_aggregate = jnp.zeros((GROUP, width), jnp.float32)
        for rotation in range(STEPS):
            holder_group = ((group_at - rotation) % groups).astype(jnp.int32)
            text_start = (holder_group * GROUP).astype(jnp.int32)
            caption_tile = lax.dynamic_slice_in_dim(caption_vector_matrix, text_start, GROUP, 0)
            entry_objective, derivative = panel_summands(picture_entries, matched_entries, caption_tile, holder_group, score_multiplier, displacement)
            objective_aggregate = objective_aggregate + entry_objective
            picture_aggregate = picture_aggregate + jnp.dot(derivative, caption_tile, preferred_element_type=jnp.float32)
            summand = score_multiplier * lax.dot_general(derivative, picture_entries, (((0,), (0,)), ((), ())), preferred_element_type=jnp.float32)
            before = lax.dynamic_slice_in_dim(caption_objective_aggregate, text_start, GROUP, 0)
            caption_objective_aggregate = lax.dynamic_update_slice_in_dim(caption_objective_aggregate, before + summand, text_start, 0)
        return caption_objective_aggregate, (objective_aggregate, score_multiplier * picture_aggregate)

    caption_objective_aggregate, (losses, image_grads) = lax.scan(visit, jnp.zeros((NROWS, width), jnp.float32), jnp.arange(groups, dtype=jnp.int32))
    return losses.reshape(NROWS), image_grads.reshape(NROWS, width), caption_objective_aggregate
```

```python
import functools

import jax
import jax.numpy as jnp
from jax import lax
from jax.experimental import pallas as pl
from jax.experimental.pallas import tpu as pltpu
from jax.sharding import PartitionSpec as P

MESH = pl.DeviceIdType.MESH
D = 1152
B = 256
HALF = 128
H = 2
SR = B // H
TR = 2 * SR
TILES = 3 * H
NIMG = 64
LN2_SERIES_LIMIT = 2.0**-6


def kernel(
    pic, cap, mat, sc, sh, loss_o, di_o, dt_o,
    img, txt, wt, wn, matm, lacc, lrecv, pi, pt, rcc,
    sx_dir, rx_dir, sx_rel, rx_rel, sy_q, ry_q,
    lsem, ag_s, ag_r, fw_s, fw_r, ty_s, ty_r, tc_s, tc_r, m_s, m_r,
    dir_s, dir_r, rel_s, rel_r, q_s, q_r, ex_s, ex_r, l_s, l_r,
):
    gi = lax.axis_index("img")
    ti = lax.axis_index("txt")
    row2 = (gi // 2) * 2
    xlo = gi % 2
    xhi = ti // 2
    core = ti % 2
    other = 1 - core
    odd = xlo == 1
    even = xlo == 0

    x_up = (row2 + 1 - xlo, ((xhi + xlo) % 2) * 2 + core)
    x_dn = (row2 + 1 - xlo, ((xhi + 1 - xlo) % 2) * 2 + core)
    x_far = (gi, (1 - xhi) * 2 + core)
    y_up = ((gi + 2) % NIMG, ti)
    y_dn = ((gi + NIMG - 2) % NIMG, ti)
    sib = (gi, xhi * 2 + other)

    scale = sc[0]
    shift = sh[0]

    barrier = pltpu.get_barrier_semaphore()
    for dev in (x_up, x_dn, x_far, y_up, y_dn, sib):
        pl.semaphore_signal(barrier, inc=1, device_id=dev, device_id_type=MESH)

    own_img = pltpu.make_async_copy(pic, img.at[pl.ds(0, B)], lsem.at[0])
    own_img.start()
    own_txt = []
    for h in range(H):
        own_txt.append(
            pltpu.make_async_copy(cap.at[h], txt.at[pl.ds(text_row(0, h, core), SR)], lsem.at[1 + h])
        )
        own_txt[h].start()
    matm[0] = jnp.broadcast_to(mat[...], (8, B))
    lacc[...] = jnp.zeros_like(lacc)
    pl.semaphore_wait(barrier, 6)

    def remote(src, dst, s, r, dev):
        return pltpu.make_async_remote_copy(
            src_ref=src, dst_ref=dst, send_sem=s, recv_sem=r, device_id=dev, device_id_type=MESH
        )

    def ag(d, half):
        rows = pl.ds(half * HALF, HALF)
        to_pos = 3 - d
        return remote(
            pic.at[rows], img.at[pl.ds(to_pos * B + half * HALF, HALF)],
            ag_s.at[d, half], ag_r.at[d, half], x_up if d == 0 else x_dn,
        )

    def fw(d):
        return remote(
            img.at[pl.ds((3 - d) * B + d * HALF, HALF)], img.at[pl.ds(B + d * HALF, HALF)],
            fw_s.at[d], fw_r.at[d], x_up if d == 0 else x_dn,
        )

    def ty(s, h):
        dst = txt.at[pl.ds(text_row(s, h, core), SR)]
        src = cap.at[h] if s == 1 else txt.at[pl.ds(text_row(s - 1, h, core), SR)]
        return remote(src, dst, ty_s.at[s - 1, h], ty_r.at[s - 1, h], y_up)

    def tc(s, h, receive=False):
        src = cap.at[h] if s == 0 else txt.at[pl.ds(text_row(s, h, core), SR)]
        dst = txt.at[pl.ds(text_row(s, h, other if receive else core), SR)]
        return remote(src, dst, tc_s.at[s, h], tc_r.at[s, h], sib)

    for d, half in ((0, 0), (1, 1), (0, 1), (1, 0)):
        ag(d, half).start()
    ty(1, 0).start()

    @pl.when(even)
    def _():
        for h in range(1, H):
            ty(1, h).start()

    for h in range(H):
        tc(0, h).start()
    far_match = remote(matm.at[0], matm.at[1], m_s, m_r, x_far)
    far_match.start()

    text_base = gi * 1024 + xhi * 512

    def scores(tile, pos):
        rows = pl.ds(pl.multiple_of(tile * TR, TR), TR)
        images = pl.ds(pl.multiple_of(pos * B, B), B)
        sims = lax.dot_general(
            txt[rows, :], img[images, :], (((1,), (1,)), ((), ())), preferred_element_type=jnp.float32
        )
        x = scale * sims + shift
        i = lax.broadcasted_iota(jnp.int32, (TR, 1), 0)
        ids = text_base + (i // SR) * B + (i % SR)
        has_label = jnp.logical_and(tile < H, pos < 2)
        ids = ids + jnp.where(has_label, tile * SR, -(1 << 30))
        label = ids == matm[jnp.minimum(pos, 1), 0:1, :]
        e = jnp.exp(-jnp.abs(x))
        u = 1.0 + e
        big = 1.0 / u
        small = e * big
        positive = x >= 0.0
        w = jnp.where(jnp.logical_xor(positive, label), big, small)
        w = jnp.where(label, -w, w).astype(jnp.bfloat16)
        series = e * (1.0 - e * (0.5 - e * (1.0 / 3.0)))
        lp = jnp.where(e < LN2_SERIES_LIMIT, series, jnp.log(u))
        loss = lp + jnp.maximum(jnp.where(label, -x, x), 0.0)
        wt[rows, images] = w
        wn[images, rows] = w.T
        lacc[pos] += jnp.sum(loss.reshape(TR // 8, 8, B), axis=0)

    def scores_loop(n, tile_of, pos_of):
        @pl.loop(0, n)
        def _(j):
            scores(tile_of(j), pos_of(j))

    def image_part(pos, base):
        cols = pl.ds(base * TR, 2 * B * 2)
        pi[pl.ds(pos * B, B)] = jnp.dot(
            wn[pl.ds(pos * B, B), cols], txt[cols, :], preferred_element_type=jnp.float32
        )

    def text_part(tile, first, count):
        rows = pl.ds(tile * TR, TR)
        ks = pl.ds(first * B, count * B)
        pt[rows] = jnp.dot(wt[rows, ks], img[ks, :], preferred_element_type=jnp.float32)

    def ex(s, h):
        tile = s * H + h
        return remote(
            pt.at[pl.ds(text_row(s, h, other), SR)], rcc.at[pl.ds(tile * SR, SR)],
            ex_s.at[s, h], ex_r.at[s, h], sib,
        )

    def chip_sum(s, h):
        tile = s * H + h
        ex(s, h).wait_recv()
        return pt[pl.ds(text_row(s, h, core), SR), :] + rcc[pl.ds(tile * SR, SR), :]

    def q(s, h):
        rows = pl.ds(((s - 1) * H + h) * SR, SR)
        return remote(sy_q.at[rows], ry_q.at[rows], q_s.at[s - 1, h], q_r.at[s - 1, h], y_dn)

    def q_send(s, h, chain=False):
        value = chip_sum(s, h)
        rows = pl.ds(((s - 1) * H + h) * SR, SR)
        if chain:
            q(2, h).wait_recv()
            value = value + ry_q[pl.ds((H + h) * SR, SR), :].astype(jnp.float32)
        sy_q[rows, :] = value.astype(jnp.bfloat16)
        q(s, h).start()

    def rel(d):
        rows = pl.ds(d * HALF, HALF)
        return remote(
            sx_rel.at[rows], rx_rel.at[rows], rel_s.at[d], rel_r.at[d], x_up if d == 0 else x_dn
        )

    def rel_send():
        sx_rel[...] = pi[pl.ds(B, B), :].astype(jnp.bfloat16)
        rel(0).start()
        rel(1).start()

    def direct(d, half):
        rows = pl.ds(d * B + half * HALF, HALF)
        return remote(
            sx_dir.at[rows], rx_dir.at[rows], dir_s.at[d, half], dir_r.at[d, half],
            x_up if d == 0 else x_dn,
        )

    def direct_send(d, half, relayed):
        rows = pl.ds(d * B + half * HALF, HALF)
        value = pi[pl.ds((2 + d) * B + half * HALF, HALF), :]
        if relayed:
            rel(d).wait_recv()
            value = value + rx_rel[pl.ds(d * HALF, HALF), :].astype(jnp.float32)
        sx_dir[rows, :] = value.astype(jnp.bfloat16)
        direct(d, half).start()

    def loss_copy(pos):
        dev = {1: x_far, 2: x_up, 3: x_dn}[pos]
        return remote(lacc.at[pos], lrecv.at[pos - 1], l_s.at[pos - 1], l_r.at[pos - 1], dev)

    def arrive(s, h):
        ty(s, h).wait_recv()
        tc(s, h).start()

    def arrive_sib(s, h):
        tc(s, h, receive=True).wait_recv()

    own_img.wait()
    for h in range(H):
        own_txt[h].wait()
    for h in range(H):
        tc(0, h, receive=True).wait_recv()
    far_match.wait_recv()
    scores_loop(H, lambda j: j, lambda j: 0)

    arrive(1, 0)

    @pl.when(odd)
    def _():
        ty(2, 0).start()
        ty(1, 1).start()

    arrive_sib(1, 0)
    scores_loop(1, lambda j: j + H, lambda j: 0)

    for d in range(2):
        for half in range(2):
            ag(d, half).wait_recv()
    fw(0).start()
    fw(1).start()

    @pl.when(even)
    def _():
        arrive(1, 1)
        scores_loop(4, lambda j: j % 2, lambda j: 2 + j // 2)
        arrive_sib(1, 1)
        scores_loop(4, lambda j: 2 + j % 2, lambda j: 2 + j // 2)
        image_part(2, 0)
        direct_send(0, 1, False)
        image_part(3, 0)
        direct_send(1, 0, False)
        scores_loop(1, lambda j: j + 3, lambda j: 0)
        fw(0).wait_recv()
        fw(1).wait_recv()
        scores_loop(4, lambda j: j, lambda j: 1)
        image_part(1, 0)
        rel_send()
        for h in range(H):
            text_part(H + h, 0, 4)
            ex(1, h).start()
        for h in range(H):
            q_send(1, h)
        for pos in (1, 2, 3):
            loss_copy(pos).start()
        for h in range(H):
            text_part(h, 0, 4)
            ex(0, h).start()
        image_part(0, 0)
        direct_send(0, 0, True)
        direct_send(1, 1, True)

    @pl.when(odd)
    def _():
        arrive(2, 0)
        scores_loop(2, lambda j: j + 2 - j, lambda j: 2 + j)
        arrive_sib(2, 0)
        scores_loop(2, lambda j: j + 4 - j, lambda j: 2 + j)
        text_part(2 * H, 2, 2)
        ex(2, 0).start()
        arrive(1, 1)
        ty(2, 1).start()
        q_send(2, 0)
        arrive_sib(1, 1)
        scores_loop(3, lambda j: j + 3 - j, lambda j: jnp.where(j == 0, 0, j + 1))
        fw(0).wait_recv()
        fw(1).wait_recv()
        scores_loop(4, lambda j: j, lambda j: 1)
        image_part(1, 0)
        rel_send()
        for h in range(H):
            text_part(H + h, 0, 4)
            ex(1, h).start()
        q_send(1, 0, chain=True)
        arrive(2, 1)
        arrive_sib(2, 1)
        scores_loop(2, lambda j: j + 5 - j, lambda j: 2 + j)
        text_part(2 * H + 1, 2, 2)
        ex(2, 1).start()
        image_part(2, H)
        direct_send(0, 1, False)
        q_send(2, 1)
        image_part(3, H)
        direct_send(1, 0, False)
        for pos in (1, 2, 3):
            loss_copy(pos).start()
        direct_send(0, 0, True)
        direct_send(1, 1, True)
        for h in range(H):
            text_part(h, 0, 2)
            ex(0, h).start()
        image_part(0, 0)
        q_send(1, 1, chain=True)

    total = lacc[0]
    for pos in (1, 2, 3):
        loss_copy(pos).wait_recv()
        total = total + lrecv[pos - 1]
    loss_o[...] = jnp.sum(total, axis=0, keepdims=True)
    for d, half in ((0, 1), (1, 0), (0, 0), (1, 1)):
        direct(d, half).wait_recv()
    di_o[...] = scale * (
        pi[pl.ds(0, B), :]
        + rx_dir[pl.ds(0, B), :].astype(jnp.float32)
        + rx_dir[pl.ds(B, B), :].astype(jnp.float32)
    )
    for h in range(H):
        own = chip_sum(0, h)
        q(1, h).wait_recv()
        dt_o[pl.ds(h * SR, SR), :] = scale * (own + ry_q[pl.ds(h * SR, SR), :].astype(jnp.float32))

    for d in range(2):
        fw(d).wait_send()
        rel(d).wait_send()
        for half in range(2):
            ag(d, half).wait_send()
            direct(d, half).wait_send()
    for h in range(H):
        ty(1, h).wait_send()
        tc(0, h).wait_send()
        tc(1, h).wait_send()
        ex(0, h).wait_send()
        ex(1, h).wait_send()
        q(1, h).wait_send()
    far_match.wait_send()
    for pos in (1, 2, 3):
        loss_copy(pos).wait_send()

    @pl.when(odd)
    def _():
        for h in range(H):
            ty(2, h).wait_send()
            tc(2, h).wait_send()
            ex(2, h).wait_send()
            q(2, h).wait_send()


def text_row(s, h, core):
    return pl.multiple_of(((s * H + h) * 2 + core) * SR, SR)


def body(pic, cap, mat, sc, sh):
    any_spec = pl.BlockSpec(memory_space=pl.ANY)
    vmem = pl.BlockSpec(memory_space=pltpu.VMEM)
    smem = pl.BlockSpec(memory_space=pltpu.SMEM)
    f32, bf16 = jnp.float32, jnp.bfloat16
    dma = pltpu.SemaphoreType.DMA
    loss, di, dt = pl.pallas_call(
        kernel,
        name="band",
        out_shape=(
            jax.ShapeDtypeStruct((1, B), f32),
            jax.ShapeDtypeStruct((B, D), f32),
            jax.ShapeDtypeStruct((B, D), f32),
        ),
        in_specs=[any_spec, any_spec, vmem, smem, smem],
        out_specs=(vmem, vmem, vmem),
        scratch_shapes=[
            pltpu.VMEM((4 * B, D), bf16),
            pltpu.VMEM((TILES * TR, D), bf16),
            pltpu.VMEM((TILES * TR, 4 * B), bf16),
            pltpu.VMEM((4 * B, TILES * TR), bf16),
            pltpu.VMEM((2, 8, B), jnp.int32),
            pltpu.VMEM((4, 8, B), f32),
            pltpu.VMEM((3, 8, B), f32),
            pltpu.VMEM((4 * B, D), f32),
            pltpu.VMEM((TILES * TR, D), f32),
            pltpu.VMEM((TILES * SR, D), f32),
            pltpu.VMEM((2 * B, D), bf16),
            pltpu.VMEM((2 * B, D), bf16),
            pltpu.VMEM((B, D), bf16),
            pltpu.VMEM((B, D), bf16),
            pltpu.VMEM((2 * B, D), bf16),
            pltpu.VMEM((2 * B, D), bf16),
            dma((1 + H,)),
            dma((2, 2)), dma((2, 2)),
            dma((2,)), dma((2,)),
            dma((2, H)), dma((2, H)),
            dma((3, H)), dma((3, H)),
            dma, dma,
            dma((2, 2)), dma((2, 2)),
            dma((2,)), dma((2,)),
            dma((2, H)), dma((2, H)),
            dma((3, H)), dma((3, H)),
            dma((3,)), dma((3,)),
        ],
        compiler_params=pltpu.CompilerParams(
            collective_id=0, has_side_effects=True, vmem_limit_bytes=56 * 2**20
        ),
        cost_estimate=pl.CostEstimate(flops=7247757312, bytes_accessed=3600000, transcendentals=3145728),
    )(pic, cap.reshape(H, SR, D), mat.reshape(1, B), sc, sh)
    return loss.reshape(B), di, dt


def solution(mesh):
    return jax.shard_map(
        body,
        mesh=mesh,
        in_specs=(P(("img", "txt"), None), P(("img", "txt"), None), P(("img", "txt")), P(), P()),
        out_specs=(P(("img", "txt")), P(("img", "txt"), None), P(("img", "txt"), None)),
        check_vma=False,
    )
```

```python
import functools

import jax
import jax.numpy as jnp
from jax import lax
from jax.experimental import pallas as pl
from jax.experimental.pallas import tpu as pltpu
from jax.sharding import PartitionSpec as P

MESH = pl.DeviceIdType.MESH
D = 1152
B = 256
HALF = 128
H = 4
SR = B // H
TR = 2 * SR
TILES = 3 * H
NIMG = 64
LOG2E = 1.4426950408889634
LN2 = 0.6931471805599453
SERIES_LIMIT = 2.0**-6


def kernel(
    pic, cap, mat, sc, sh, loss_o, pi_o, rx_late, q0_o, ry_o,
    scal, img, txt, wt, wn, matm, lacc, lrecv, pi, pt, rcc,
    sx_dir, rx_pure, sx_rel, rx_rel, sy_q, ry_q2,
    lsem, ag_s, ag_r, fw_s, fw_r, ty_s, ty_r, tc_s, tc_r, m_s, m_r,
    dir_s, dir_r, rel_s, rel_r, q_s, q_r, ex_s, ex_r, l_s, l_r, o_s,
):
    gi = lax.axis_index("img")
    ti = lax.axis_index("txt")
    row2 = (gi // 2) * 2
    xlo = gi % 2
    xhi = ti // 2
    core = ti % 2
    other = 1 - core
    odd = xlo == 1
    even = xlo == 0

    x_up = (row2 + 1 - xlo, ((xhi + xlo) % 2) * 2 + core)
    x_dn = (row2 + 1 - xlo, ((xhi + 1 - xlo) % 2) * 2 + core)
    x_far = (gi, (1 - xhi) * 2 + core)
    y_up = ((gi + 2) % NIMG, ti)
    y_dn = ((gi + NIMG - 2) % NIMG, ti)
    sib = (gi, xhi * 2 + other)

    barrier = pltpu.get_barrier_semaphore()
    for dev in (x_up, x_dn, x_far, y_up, y_dn, sib):
        pl.semaphore_signal(barrier, inc=1, device_id=dev, device_id_type=MESH)

    own_img = pltpu.make_async_copy(pic, img.at[pl.ds(0, B)], lsem.at[0])
    own_img.start()
    own_txt = []
    for h in range(H):
        own_txt.append(
            pltpu.make_async_copy(cap.at[h], txt.at[pl.ds(text_row(0, h, core), SR)], lsem.at[1 + h])
        )
        own_txt[h].start()
    small = [
        pltpu.make_async_copy(sc, scal.at[0], lsem.at[1 + H]),
        pltpu.make_async_copy(sh, scal.at[1], lsem.at[2 + H]),
        pltpu.make_async_copy(mat, matm.at[0], lsem.at[3 + H]),
    ]
    for copy in small:
        copy.start()
    lacc[...] = jnp.zeros_like(lacc)
    pl.semaphore_wait(barrier, 6)

    def remote(src, dst, s, r, dev):
        return pltpu.make_async_remote_copy(
            src_ref=src, dst_ref=dst, send_sem=s, recv_sem=r, device_id=dev, device_id_type=MESH
        )

    def ag(d, half):
        rows = pl.ds(half * HALF, HALF)
        to_pos = 3 - d
        return remote(
            pic.at[rows], img.at[pl.ds(to_pos * B + half * HALF, HALF)],
            ag_s.at[d, half], ag_r.at[d, half], x_up if d == 0 else x_dn,
        )

    def fw(d):
        return remote(
            img.at[pl.ds((3 - d) * B + d * HALF, HALF)], img.at[pl.ds(B + d * HALF, HALF)],
            fw_s.at[d], fw_r.at[d], x_up if d == 0 else x_dn,
        )

    def ty(s, h):
        dst = txt.at[pl.ds(text_row(s, h, core), SR)]
        src = cap.at[h] if s == 1 else txt.at[pl.ds(text_row(s - 1, h, core), SR)]
        return remote(src, dst, ty_s.at[s - 1, h], ty_r.at[s - 1, h], y_up)

    def tc(s, h, receive=False):
        src = cap.at[h] if s == 0 else txt.at[pl.ds(text_row(s, h, core), SR)]
        dst = txt.at[pl.ds(text_row(s, h, other if receive else core), SR)]
        return remote(src, dst, tc_s.at[s, h], tc_r.at[s, h], sib)

    ty(1, 0).start()
    far_match = remote(mat, matm.at[1], m_s, m_r, x_far)
    far_match.start()
    for h in range(H):
        tc(0, h).start()
    ag(0, 0).start()
    ag(1, 1).start()
    ty(1, 1).start()
    ag(0, 1).start()
    ag(1, 0).start()

    @pl.when(even)
    def _():
        for h in range(2, H):
            ty(1, h).start()

    for copy in small:
        copy.wait()
    scale = scal[0, 0] * LOG2E
    shift = scal[1, 0] * LOG2E
    text_base = gi * 1024 + xhi * 512

    def scores(tile, count, pos, labelled):
        n = count * TR
        rows = pl.ds(pl.multiple_of(tile * TR, TR), n)
        images = pl.ds(pl.multiple_of(pos * B, B), B)
        sims = lax.dot_general(
            txt[rows, :], img[images, :], (((1,), (1,)), ((), ())), preferred_element_type=jnp.float32
        )
        x = scale * sims + shift
        e = jnp.exp2(-jnp.abs(x))
        u = 1.0 + e
        r = pltpu.reciprocal(u, approx=True)
        big = r * (2.0 - u * r)
        small = e * big
        series = e * (LOG2E - e * (LOG2E / 2 - e * (LOG2E / 3)))
        lp = jnp.where(e < SERIES_LIMIT, series, jnp.log2(u))
        positive = x >= 0.0
        if labelled:
            i = lax.broadcasted_iota(jnp.int32, (n, 1), 0)
            ids = text_base + ((i % TR) // SR) * B + (i // TR) * SR + i % SR
            label = ids == matm[pos]
            w = jnp.where(jnp.logical_xor(positive, label), big, small)
            w = jnp.where(label, -w, w)
            loss = lp + jnp.maximum(jnp.where(label, -x, x), 0.0)
        else:
            w = jnp.where(positive, big, small)
            loss = lp + jnp.maximum(x, 0.0)
        w = w.astype(jnp.bfloat16)
        wt[rows, images] = w
        wn[images, rows] = w.T
        lacc[pos] += jnp.sum(loss.reshape(n // 8, 8, B), axis=0)

    def scores_loop(n, tile_of, count, pos_of):
        @pl.loop(0, n)
        def _(j):
            scores(tile_of(j), count, pos_of(j), False)

    def own_scores(pos):
        scores(0, H, pos, True)

    def image_part(pos, tile, count, add=False):
        cols = pl.ds(tile * TR, count * TR)
        part = jnp.dot(wn[pl.ds(pos * B, B), cols], txt[cols, :], preferred_element_type=jnp.float32)
        if add:
            part = part + pi[pl.ds(pos * B, B)]
        pi[pl.ds(pos * B, B)] = part

    def text_part(s, h, count, first=0, blocks=4):
        rows = pl.ds((s * H + h) * TR, count * TR)
        ks = pl.ds(first * B, blocks * B)
        pt[rows] = jnp.dot(wt[rows, ks], img[ks, :], preferred_element_type=jnp.float32)
        for k in range(h, h + count):
            ex(s, k).start()

    def ex(s, h):
        tile = s * H + h
        return remote(
            pt.at[pl.ds(text_row(s, h, other), SR)], rcc.at[pl.ds(tile * SR, SR)],
            ex_s.at[s, h], ex_r.at[s, h], sib,
        )

    def chip_sum(s, h):
        tile = s * H + h
        ex(s, h).wait_recv()
        return pt[pl.ds(text_row(s, h, core), SR), :] + rcc[pl.ds(tile * SR, SR), :]

    def q(s, h):
        rows = pl.ds(h * SR, SR)
        dst = ry_o if s == 1 else ry_q2
        return remote(
            sy_q.at[pl.ds(((s - 1) * H + h) * SR, SR)], dst.at[rows], q_s.at[s - 1, h], q_r.at[s - 1, h], y_dn
        )

    def q_send(s, h, chain=False):
        value = chip_sum(s, h)
        if chain:
            q(2, h).wait_recv()
            value = value + ry_q2[pl.ds(h * SR, SR), :].astype(jnp.float32)
        sy_q[pl.ds(((s - 1) * H + h) * SR, SR), :] = value.astype(jnp.bfloat16)
        q(s, h).start()

    def rel(d):
        rows = pl.ds(d * HALF, HALF)
        return remote(
            sx_rel.at[rows], rx_rel.at[rows], rel_s.at[d], rel_r.at[d], x_up if d == 0 else x_dn
        )

    def rel_send():
        sx_rel[...] = pi[pl.ds(B, B), :].astype(jnp.bfloat16)
        rel(0).start()
        rel(1).start()

    def direct(d, half):
        rows = pl.ds(half * HALF, HALF)
        return remote(
            sx_dir.at[pl.ds(d * B + half * HALF, HALF)], (rx_late if d == half else rx_pure).at[rows],
            dir_s.at[d, half], dir_r.at[d, half], x_up if d == 0 else x_dn,
        )

    def direct_send(d, relayed):
        half = d if relayed else 1 - d
        value = pi[pl.ds((2 + d) * B + half * HALF, HALF), :]
        if relayed:
            rel(d).wait_recv()
            value = value + rx_rel[pl.ds(d * HALF, HALF), :].astype(jnp.float32)
        sx_dir[pl.ds(d * B + half * HALF, HALF), :] = value.astype(jnp.bfloat16)
        direct(d, half).start()

    def loss_copy(pos):
        dev = {1: x_far, 2: x_up, 3: x_dn}[pos]
        return remote(lacc.at[pos], lrecv.at[pos - 1], l_s.at[pos - 1], l_r.at[pos - 1], dev)

    def arrive(s, h):
        ty(s, h).wait_recv()
        tc(s, h).start()

    def arrive_sib(s, h):
        tc(s, h, receive=True).wait_recv()

    def pass_on(h):
        ty(2, h).start()
        if h + 2 < H:
            ty(1, h + 2).start()

    def hand_on_images():
        for d in range(2):
            ag(d, d).wait_recv()
            fw(d).start()

    def neighbours():
        for d in range(2):
            ag(d, 1 - d).wait_recv()

    def far():
        fw(0).wait_recv()
        fw(1).wait_recv()

    own_img.wait()
    for h in range(H):
        own_txt[h].wait()
    for h in range(H):
        tc(0, h, receive=True).wait_recv()
    far_match.wait_recv()
    own_scores(0)

    @pl.when(even)
    def _():
        arrive(1, 0)
        arrive(1, 1)
        arrive_sib(1, 0)
        arrive_sib(1, 1)
        scores_loop(1, lambda j: H + j, 2, lambda j: 0)
        arrive(1, 2)
        hand_on_images()
        neighbours()
        arrive(1, 3)
        scores_loop(2, lambda j: 0, H, lambda j: 2 + j)
        arrive_sib(1, 2)
        arrive_sib(1, 3)
        scores_loop(2, lambda j: H, H, lambda j: 2 + j)
        image_part(2, 0, 2 * H)
        direct_send(0, False)
        image_part(3, 0, 2 * H)
        direct_send(1, False)
        scores_loop(1, lambda j: H + 2 + j, 2, lambda j: 0)
        far()
        scores_loop(1, lambda j: H + j, H, lambda j: 1)
        text_part(1, 0, 2)
        text_part(1, 2, 2)
        q_send(1, 0)
        q_send(1, 1)
        own_scores(1)
        q_send(1, 2)
        q_send(1, 3)
        image_part(1, 0, 2 * H)
        rel_send()
        for pos in (1, 2, 3):
            loss_copy(pos).start()
        image_part(0, 0, 2 * H)
        text_part(0, 0, H)
        direct_send(0, True)
        direct_send(1, True)

    @pl.when(odd)
    def _():
        arrive(1, 0)
        pass_on(0)
        arrive(1, 1)
        pass_on(1)
        arrive_sib(1, 0)
        arrive_sib(1, 1)
        scores_loop(1, lambda j: H + j, 2, lambda j: 0)
        arrive(2, 0)
        hand_on_images()
        arrive_sib(2, 0)
        neighbours()
        scores_loop(2, lambda j: 2 * H, 1, lambda j: 2 + j)
        text_part(2, 0, 1, 2, 2)
        arrive(1, 2)
        pass_on(2)
        scores_loop(2, lambda j: H, 2, lambda j: 2 + j)
        q_send(2, 0)
        arrive(2, 1)
        arrive_sib(2, 1)
        scores_loop(2, lambda j: 2 * H + 1, 1, lambda j: 2 + j)
        text_part(2, 1, 1, 2, 2)
        far()
        own_scores(1)
        q_send(2, 1)
        arrive(1, 3)
        pass_on(3)
        arrive_sib(1, 2)
        arrive_sib(1, 3)
        scores_loop(1, lambda j: H + j, H, lambda j: 1)
        image_part(1, 0, 2 * H)
        rel_send()
        text_part(1, 0, 2)
        scores_loop(3, lambda j: H + 2, 2, lambda j: j + jnp.minimum(j, 1))
        arrive(2, 2)
        q_send(1, 0, chain=True)
        q_send(1, 1, chain=True)
        image_part(2, H, H)
        image_part(3, H, H)
        arrive(2, 3)
        text_part(1, 2, 2)
        arrive_sib(2, 2)
        arrive_sib(2, 3)
        scores_loop(2, lambda j: 2 * H + 2, 2, lambda j: 2 + j)
        image_part(2, 2 * H, H, add=True)
        direct_send(0, False)
        image_part(3, 2 * H, H, add=True)
        direct_send(1, False)
        text_part(2, 2, 2, 2, 2)
        for pos in (1, 2, 3):
            loss_copy(pos).start()
        image_part(0, 0, 2 * H)
        q_send(2, 2)
        q_send(2, 3)
        text_part(0, 0, H, 0, 2)
        q_send(1, 2, chain=True)
        direct_send(0, True)
        direct_send(1, True)
        q_send(1, 3, chain=True)

    for h in range(H):
        rows = pl.ds(text_row(0, h, core), SR)
        pt[rows, :] = chip_sum(0, h)
    q0_out = [
        pltpu.make_async_copy(pt.at[pl.ds(text_row(0, h, core), SR)], q0_o.at[pl.ds(h * SR, SR)], o_s.at[1 + h])
        for h in range(H)
    ]
    for h in range(H):
        q0_out[h].start()
    total = lacc[0]
    for pos in (1, 2, 3):
        loss_copy(pos).wait_recv()
        total = total + lrecv[pos - 1]
    loss_o[...] = total
    direct(0, 1).wait_recv()
    direct(1, 0).wait_recv()
    pi[pl.ds(0, B), :] += rx_pure[...].astype(jnp.float32)
    pi_out = pltpu.make_async_copy(pi.at[pl.ds(0, B)], pi_o, o_s.at[0])
    pi_out.start()

    for d in range(2):
        fw(d).wait_send()
        rel(d).wait_send()
        for half in range(2):
            ag(d, half).wait_send()
    for h in range(H):
        ty(1, h).wait_send()
        tc(0, h).wait_send()
        tc(1, h).wait_send()
        ex(0, h).wait_send()
        ex(1, h).wait_send()
    far_match.wait_send()
    for pos in (1, 2, 3):
        loss_copy(pos).wait_send()

    @pl.when(odd)
    def _():
        for h in range(H):
            ty(2, h).wait_send()
            tc(2, h).wait_send()
            ex(2, h).wait_send()
            q(2, h).wait_send()

    for h in range(H):
        q0_out[h].wait()
    pi_out.wait()
    for d in range(2):
        for half in range(2):
            direct(d, half).wait_send()
        direct(d, d).wait_recv()
    for h in range(H):
        q(1, h).wait()


def finish(scale, loss, pi, late, q0, ry, loss_o, di_o, dt_o):
    s = scale[0]
    di_o[...] = s * (pi[...] + late[...].astype(jnp.float32))
    dt_o[...] = s * (q0[...] + ry[...].astype(jnp.float32))
    loss_o[...] = LN2 * jnp.sum(loss[...], axis=0, keepdims=True)


def text_row(s, h, core):
    return pl.multiple_of(((s * H + h) * 2 + core) * SR, SR)


def body(pic, cap, mat, sc, sh):
    any_spec = pl.BlockSpec(memory_space=pl.ANY)
    vmem = pl.BlockSpec(memory_space=pltpu.VMEM)
    smem = pl.BlockSpec(memory_space=pltpu.SMEM)
    f32, bf16 = jnp.float32, jnp.bfloat16
    dma = pltpu.SemaphoreType.DMA
    parts = pl.pallas_call(
        kernel,
        name="band",
        out_shape=(
            jax.ShapeDtypeStruct((8, B), f32),
            jax.ShapeDtypeStruct((B, D), f32),
            jax.ShapeDtypeStruct((B, D), bf16),
            jax.ShapeDtypeStruct((B, D), f32),
            jax.ShapeDtypeStruct((B, D), bf16),
        ),
        in_specs=[any_spec] * 5,
        out_specs=(vmem, any_spec, any_spec, any_spec, any_spec),
        scratch_shapes=[
            pltpu.SMEM((2, 1), f32),
            pltpu.VMEM((4 * B, D), bf16),
            pltpu.VMEM((TILES * TR, D), bf16),
            pltpu.VMEM((TILES * TR, 4 * B), bf16),
            pltpu.VMEM((4 * B, TILES * TR), bf16),
            pltpu.VMEM((2, 1, B), jnp.int32),
            pltpu.VMEM((4, 8, B), f32),
            pltpu.VMEM((3, 8, B), f32),
            pltpu.VMEM((4 * B, D), f32),
            pltpu.VMEM((TILES * TR, D), f32),
            pltpu.VMEM((TILES * SR, D), f32),
            pltpu.VMEM((2 * B, D), bf16),
            pltpu.VMEM((B, D), bf16),
            pltpu.VMEM((B, D), bf16),
            pltpu.VMEM((B, D), bf16),
            pltpu.VMEM((2 * B, D), bf16),
            pltpu.VMEM((B, D), bf16),
            dma((4 + H,)),
            dma((2, 2)), dma((2, 2)),
            dma((2,)), dma((2,)),
            dma((2, H)), dma((2, H)),
            dma((3, H)), dma((3, H)),
            dma, dma,
            dma((2, 2)), dma((2, 2)),
            dma((2,)), dma((2,)),
            dma((2, H)), dma((2, H)),
            dma((3, H)), dma((3, H)),
            dma((3,)), dma((3,)),
            dma((1 + H,)),
        ],
        compiler_params=pltpu.CompilerParams(
            collective_id=0, has_side_effects=True, vmem_limit_bytes=56 * 2**20
        ),
        cost_estimate=pl.CostEstimate(flops=7247757312, bytes_accessed=3600000, transcendentals=3145728),
    )(pic, cap.reshape(H, SR, D), mat.reshape(1, B), sc, sh)
    blocks = 2
    rows = pl.BlockSpec((B // blocks, D), lambda i: (i, 0))
    loss, di, dt = pl.pallas_call(
        finish,
        name="finish",
        grid=(blocks,),
        out_shape=(
            jax.ShapeDtypeStruct((1, B), f32),
            jax.ShapeDtypeStruct((B, D), f32),
            jax.ShapeDtypeStruct((B, D), f32),
        ),
        in_specs=[smem, pl.BlockSpec((8, B), lambda i: (0, 0)), rows, rows, rows, rows],
        out_specs=(pl.BlockSpec((1, B), lambda i: (0, 0)), rows, rows),
    )(sc, *parts)
    return loss.reshape(B), di, dt


def solution(mesh):
    return jax.shard_map(
        body,
        mesh=mesh,
        in_specs=(P(("img", "txt"), None), P(("img", "txt"), None), P(("img", "txt")), P(), P()),
        out_specs=(P(("img", "txt")), P(("img", "txt"), None), P(("img", "txt"), None)),
        check_vma=False,
    )
```

```python
import functools

import jax
import jax.numpy as jnp
from jax import lax
from jax.experimental import pallas as pl
from jax.experimental.pallas import tpu as pltpu
from jax.sharding import PartitionSpec as P

MESH = pl.DeviceIdType.MESH
D = 1152
B = 256
HALF = 128
H = 4
SR = B // H
TR = 2 * SR
TILES = 3 * H
NIMG = 64
LOG2E = 1.4426950408889634
LN2 = 0.6931471805599453
SERIES_LIMIT = 2.0**-6


def kernel(
    pic, cap, mat, sc, sh, loss_o, pi_o, rx_late, q0_o, ry_o,
    scal, img, txt, wt, wn, matm, lacc, lrecv, pi, pt, rcc,
    sx_dir, rx_pure, sx_rel, rx_rel, sy_q, ry_q2, tr, tq, rq,
    lsem, ag_s, ag_r, fw_s, fw_r, ty_s, ty_r, tc_s, tc_r, m_s, m_r,
    dir_s, dir_r, rel_s, rel_r, q_s, q_r, ex_s, ex_r, l_s, l_r, o_s,
    tr_s, tr_r, tf_s, tf_r, tq_s, tq_r, tg_s, tg_r,
):
    gi = lax.axis_index("img")
    ti = lax.axis_index("txt")
    row2 = (gi // 2) * 2
    xlo = gi % 2
    xhi = ti // 2
    core = ti % 2
    other = 1 - core
    odd = xlo == 1
    even = xlo == 0

    x_up = (row2 + 1 - xlo, ((xhi + xlo) % 2) * 2 + core)
    x_dn = (row2 + 1 - xlo, ((xhi + 1 - xlo) % 2) * 2 + core)
    x_far = (gi, (1 - xhi) * 2 + core)
    y_up = ((gi + 2) % NIMG, ti)
    y_dn = ((gi + NIMG - 2) % NIMG, ti)
    sib = (gi, xhi * 2 + other)
    y, z = (gi // 2) % 4, gi // 8
    above, below = (y + 1) % 4, (y + 3) % 4

    def at(yy, zz):
        return ((zz + 8) % 8 * 8 + yy * 2 + xlo, ti)

    far_up, far_dn = at(above, z), at(below, z)
    hand_to, hand_from = at(below, z + above // 2), at(above, z - 1 + y // 2)
    home_to, home_from = at(above, z - 1 + below // 2), at(below, z + 1 - ((y + 2) % 4) // 2)

    barrier = pltpu.get_barrier_semaphore()
    partners = (x_up, x_dn, x_far, y_up, y_dn, sib)
    partners += (far_up, far_dn, hand_to, hand_from, home_to, home_from)
    for dev in partners:
        pl.semaphore_signal(barrier, inc=1, device_id=dev, device_id_type=MESH)

    own_img = pltpu.make_async_copy(pic, img.at[pl.ds(0, B)], lsem.at[0])
    own_img.start()
    own_txt = []
    for h in range(H):
        own_txt.append(
            pltpu.make_async_copy(cap.at[h], txt.at[pl.ds(text_row(0, h, core), SR)], lsem.at[1 + h])
        )
        own_txt[h].start()
    small = [
        pltpu.make_async_copy(sc, scal.at[0], lsem.at[1 + H]),
        pltpu.make_async_copy(sh, scal.at[1], lsem.at[2 + H]),
        pltpu.make_async_copy(mat, matm.at[0], lsem.at[3 + H]),
    ]
    for copy in small:
        copy.start()
    lacc[...] = jnp.zeros_like(lacc)
    pl.semaphore_wait(barrier, len(partners))

    def remote(src, dst, s, r, dev):
        return pltpu.make_async_remote_copy(
            src_ref=src, dst_ref=dst, send_sem=s, recv_sem=r, device_id=dev, device_id_type=MESH
        )

    def ag(d, half):
        rows = pl.ds(half * HALF, HALF)
        to_pos = 3 - d
        return remote(
            pic.at[rows], img.at[pl.ds(to_pos * B + half * HALF, HALF)],
            ag_s.at[d, half], ag_r.at[d, half], x_up if d == 0 else x_dn,
        )

    def fw(d):
        return remote(
            img.at[pl.ds((3 - d) * B + d * HALF, HALF)], img.at[pl.ds(B + d * HALF, HALF)],
            fw_s.at[d], fw_r.at[d], x_up if d == 0 else x_dn,
        )

    def ty(s, h):
        dst = txt.at[pl.ds(text_row(s, h, core), SR)]
        src = cap.at[h] if s == 1 else txt.at[pl.ds(text_row(s - 1, h, core), SR)]
        return remote(src, dst, ty_s.at[s - 1, h], ty_r.at[s - 1, h], y_up)

    def tc(s, h, receive=False):
        src = cap.at[h] if s == 0 else txt.at[pl.ds(text_row(s, h, core), SR)]
        dst = txt.at[pl.ds(text_row(s, h, other if receive else core), SR)]
        return remote(src, dst, tc_s.at[s, h], tc_r.at[s, h], sib)

    def there(i):
        return remote(cap.at[H // 2 + i], tr.at[pl.ds(i * SR, SR)], tr_s.at[i], tr_r.at[i], far_dn)

    def onward(i):
        dst = txt.at[pl.ds(text_row(2, H // 2 + i, core), SR)]
        return remote(tr.at[pl.ds(i * SR, SR)], dst, tf_s.at[i], tf_r.at[i], hand_to)

    far_match = remote(mat, matm.at[1], m_s, m_r, x_far)
    far_match.start()
    ty(1, 0).start()
    pl.when(odd)(there(0).start)
    ag(0, 0).start()
    ag(1, 1).start()
    pl.when(odd)(there(1).start)
    for h in range(H):
        tc(0, h).start()
    ty(1, 1).start()
    ag(0, 1).start()
    ag(1, 0).start()
    for h in range(2, H):
        ty(1, h).start()

    for copy in small:
        copy.wait()
    scale = scal[0, 0] * LOG2E
    shift = scal[1, 0] * LOG2E
    text_base = gi * 1024 + xhi * 512

    def scores(tile, count, pos, labelled):
        n = count * TR
        rows = pl.ds(pl.multiple_of(tile * TR, TR), n)
        images = pl.ds(pl.multiple_of(pos * B, B), B)
        sims = lax.dot_general(
            txt[rows, :], img[images, :], (((1,), (1,)), ((), ())), preferred_element_type=jnp.float32
        )
        x = scale * sims + shift
        e = jnp.exp2(-jnp.abs(x))
        u = 1.0 + e
        r = pltpu.reciprocal(u, approx=True)
        big = r * (2.0 - u * r)
        small = e * big
        series = e * (LOG2E - e * (LOG2E / 2 - e * (LOG2E / 3)))
        lp = jnp.where(e < SERIES_LIMIT, series, jnp.log2(u))
        positive = x >= 0.0
        if labelled:
            i = lax.broadcasted_iota(jnp.int32, (n, 1), 0)
            ids = text_base + ((i % TR) // SR) * B + (i // TR) * SR + i % SR
            label = ids == matm[pos]
            w = jnp.where(jnp.logical_xor(positive, label), big, small)
            w = jnp.where(label, -w, w)
            loss = lp + jnp.maximum(jnp.where(label, -x, x), 0.0)
        else:
            w = jnp.where(positive, big, small)
            loss = lp + jnp.maximum(x, 0.0)
        w = w.astype(jnp.bfloat16)
        wt[rows, images] = w
        wn[images, rows] = w.T
        lacc[pos] += jnp.sum(loss.reshape(n // 8, 8, B), axis=0)

    def scores_loop(n, tile_of, count, pos_of):
        @pl.loop(0, n)
        def _(j):
            scores(tile_of(j), count, pos_of(j), False)

    def own_scores(pos):
        scores(0, H, pos, True)

    def image_part(pos, tile, count):
        cols = pl.ds(tile * TR, count * TR)
        pi[pl.ds(pos * B, B)] = jnp.dot(
            wn[pl.ds(pos * B, B), cols], txt[cols, :], preferred_element_type=jnp.float32
        )

    def text_part(s, h, count, first=0, blocks=4):
        rows = pl.ds((s * H + h) * TR, count * TR)
        ks = pl.ds(first * B, blocks * B)
        pt[rows] = jnp.dot(wt[rows, ks], img[ks, :], preferred_element_type=jnp.float32)
        for k in range(h, h + count):
            ex(s, k).start()

    def ex(s, h):
        tile = s * H + h
        return remote(
            pt.at[pl.ds(text_row(s, h, other), SR)], rcc.at[pl.ds(tile * SR, SR)],
            ex_s.at[s, h], ex_r.at[s, h], sib,
        )

    def chip_sum(s, h):
        tile = s * H + h
        ex(s, h).wait_recv()
        return pt[pl.ds(text_row(s, h, core), SR), :] + rcc[pl.ds(tile * SR, SR), :]

    def q(s, h):
        rows = pl.ds(h * SR, SR)
        dst = ry_o if s == 1 else ry_q2
        return remote(
            sy_q.at[pl.ds(((s - 1) * H + h) * SR, SR)], dst.at[rows], q_s.at[s - 1, h], q_r.at[s - 1, h], y_dn
        )

    def q_send(s, h, chain=False):
        value = chip_sum(s, h)
        if chain:
            q(2, h).wait_recv()
            value = value + ry_q2[pl.ds(h * SR, SR), :].astype(jnp.float32)
        sy_q[pl.ds(((s - 1) * H + h) * SR, SR), :] = value.astype(jnp.bfloat16)
        q(s, h).start()

    def back(h):
        rows = pl.ds(h * SR, SR)
        return remote(sy_q.at[pl.ds((H + h) * SR, SR)], tq.at[rows], tq_s.at[h], tq_r.at[h], far_up)

    def home(h):
        rows = pl.ds(h * SR, SR)
        return remote(tq.at[rows], rq.at[rows], tg_s.at[h], tg_r.at[h], home_to)

    def back_send(h):
        sy_q[pl.ds((H + h) * SR, SR), :] = chip_sum(2, h).astype(jnp.bfloat16)
        back(h).start()

    def home_send(h):
        back(h).wait_recv()
        home(h).start()

    def rel(d):
        rows = pl.ds(d * HALF, HALF)
        return remote(
            sx_rel.at[rows], rx_rel.at[rows], rel_s.at[d], rel_r.at[d], x_up if d == 0 else x_dn
        )

    def rel_send():
        sx_rel[...] = pi[pl.ds(B, B), :].astype(jnp.bfloat16)
        rel(0).start()
        rel(1).start()

    def direct(d, half):
        rows = pl.ds(half * HALF, HALF)
        return remote(
            sx_dir.at[pl.ds(d * B + half * HALF, HALF)], (rx_late if d == half else rx_pure).at[rows],
            dir_s.at[d, half], dir_r.at[d, half], x_up if d == 0 else x_dn,
        )

    def direct_send(d, relayed):
        half = d if relayed else 1 - d
        value = pi[pl.ds((2 + d) * B + half * HALF, HALF), :]
        if relayed:
            rel(d).wait_recv()
            value = value + rx_rel[pl.ds(d * HALF, HALF), :].astype(jnp.float32)
        sx_dir[pl.ds(d * B + half * HALF, HALF), :] = value.astype(jnp.bfloat16)
        direct(d, half).start()

    def loss_copy(pos):
        dev = {1: x_far, 2: x_up, 3: x_dn}[pos]
        return remote(lacc.at[pos], lrecv.at[pos - 1], l_s.at[pos - 1], l_r.at[pos - 1], dev)

    def arrive(s, h):
        (onward(h - H // 2) if s == 2 and h >= H // 2 else ty(s, h)).wait_recv()
        tc(s, h).start()

    def arrive_sib(s, h):
        tc(s, h, receive=True).wait_recv()

    def pass_on(h):
        there(h).wait_recv()
        onward(h).start()

    def hand_on_images():
        for d in range(2):
            ag(d, d).wait_recv()
            fw(d).start()

    def neighbours():
        for d in range(2):
            ag(d, 1 - d).wait_recv()

    def far():
        fw(0).wait_recv()
        fw(1).wait_recv()

    own_img.wait()
    for h in range(H):
        own_txt[h].wait()
    for h in range(H):
        tc(0, h, receive=True).wait_recv()
    far_match.wait_recv()
    own_scores(0)

    @pl.when(even)
    def _():
        arrive(1, 0)
        arrive(1, 1)
        hand_on_images()
        arrive_sib(1, 0)
        arrive_sib(1, 1)
        scores_loop(1, lambda j: H + j, 2, lambda j: 0)
        arrive(1, 2)
        neighbours()
        arrive(1, 3)
        scores_loop(2, lambda j: 0, H, lambda j: 2 + j)
        arrive_sib(1, 2)
        arrive_sib(1, 3)
        scores_loop(2, lambda j: H, H, lambda j: 2 + j)
        image_part(2, 0, 2 * H)
        direct_send(0, False)
        image_part(3, 0, 2 * H)
        direct_send(1, False)
        scores_loop(1, lambda j: H + 2 + j, 2, lambda j: 0)
        far()
        scores_loop(1, lambda j: H + j, H, lambda j: 1)
        own_scores(1)
        image_part(1, 0, 2 * H)
        rel_send()
        text_part(1, 0, 2)
        for pos in (1, 2, 3):
            loss_copy(pos).start()
        text_part(1, 2, 2)
        q_send(1, 0)
        q_send(1, 1)
        text_part(0, 0, 2)
        q_send(1, 2)
        q_send(1, 3)
        text_part(0, 2, 2)
        image_part(0, 0, 2 * H)
        direct_send(0, True)
        direct_send(1, True)

    @pl.when(odd)
    def _():
        arrive(1, 0)
        ty(2, 0).start()
        arrive(1, 1)
        ty(2, 1).start()
        hand_on_images()
        arrive_sib(1, 0)
        arrive_sib(1, 1)
        scores_loop(1, lambda j: H + j, 2, lambda j: 0)
        pass_on(0)
        arrive(1, 2)
        pass_on(1)
        arrive(2, 2)
        neighbours()
        arrive(1, 3)
        scores_loop(2, lambda j: H, 2, lambda j: 2 + j)
        arrive_sib(1, 2)
        arrive_sib(1, 3)
        scores_loop(3, lambda j: H + 2, 2, lambda j: j + jnp.minimum(j, 1))
        arrive(2, 3)
        arrive(2, 0)
        arrive_sib(2, 2)
        scores_loop(2, lambda j: 2 * H + 2, 1, lambda j: 2 + j)
        text_part(2, 2, 1, 2, 2)
        far()
        own_scores(1)
        q_send(2, 2)
        arrive(2, 1)
        scores_loop(1, lambda j: H + j, H, lambda j: 1)
        image_part(1, 0, 2 * H)
        rel_send()
        text_part(1, 0, 2)
        arrive_sib(2, 3)
        scores_loop(2, lambda j: 2 * H + 3, 1, lambda j: 2 + j)
        arrive_sib(2, 0)
        arrive_sib(2, 1)
        q_send(1, 0)
        scores_loop(2, lambda j: 2 * H, 2, lambda j: 2 + j)
        q_send(1, 1)
        text_part(2, 0, 2, 2, 2)
        image_part(2, H, 2 * H)
        direct_send(0, False)
        back_send(0)
        back_send(1)
        image_part(3, H, 2 * H)
        direct_send(1, False)
        text_part(2, 3, 1, 2, 2)
        text_part(1, 2, 2)
        q_send(2, 3)
        for pos in (1, 2, 3):
            loss_copy(pos).start()
        image_part(0, 0, 2 * H)
        text_part(0, 0, 2, 0, 2)
        text_part(0, 2, 2, 0, 2)
        q_send(1, 2, chain=True)
        home_send(0)
        direct_send(0, True)
        direct_send(1, True)
        home_send(1)
        q_send(1, 3, chain=True)

    for h in range(H):
        rows = pl.ds(text_row(0, h, core), SR)
        pt[rows, :] = chip_sum(0, h)

    @pl.when(odd)
    def _():
        for h in range(H // 2):
            rows = pl.ds(text_row(0, h, core), SR)
            home(h).wait_recv()
            pt[rows, :] += rq[pl.ds(h * SR, SR), :].astype(jnp.float32)

    q0_out = [
        pltpu.make_async_copy(pt.at[pl.ds(text_row(0, h, core), SR)], q0_o.at[pl.ds(h * SR, SR)], o_s.at[1 + h])
        for h in range(H)
    ]
    for h in range(H):
        q0_out[h].start()
    total = lacc[0]
    for pos in (1, 2, 3):
        loss_copy(pos).wait_recv()
        total = total + lrecv[pos - 1]
    loss_o[...] = total
    direct(0, 1).wait_recv()
    direct(1, 0).wait_recv()
    pi[pl.ds(0, B), :] += rx_pure[...].astype(jnp.float32)
    pi_out = pltpu.make_async_copy(pi.at[pl.ds(0, B)], pi_o, o_s.at[0])
    pi_out.start()

    for d in range(2):
        fw(d).wait_send()
        rel(d).wait_send()
        for half in range(2):
            ag(d, half).wait_send()
    for h in range(H):
        ty(1, h).wait_send()
        tc(0, h).wait_send()
        tc(1, h).wait_send()
        ex(0, h).wait_send()
        ex(1, h).wait_send()
    far_match.wait_send()
    for pos in (1, 2, 3):
        loss_copy(pos).wait_send()

    @pl.when(odd)
    def _():
        for h in range(H):
            tc(2, h).wait_send()
            ex(2, h).wait_send()
        for h in range(H // 2):
            ty(2, h).wait_send()
            there(h).wait_send()
            onward(h).wait_send()
            q(2, H // 2 + h).wait_send()
            back(h).wait_send()
            home(h).wait_send()

    for h in range(H):
        q0_out[h].wait()
    pi_out.wait()
    for d in range(2):
        for half in range(2):
            direct(d, half).wait_send()
        direct(d, d).wait_recv()
    for h in range(H):
        q(1, h).wait()


def finish(scale, loss, pi, late, q0, ry, loss_o, di_o, dt_o):
    s = scale[0]
    di_o[...] = s * (pi[...] + late[...].astype(jnp.float32))
    dt_o[...] = s * (q0[...] + ry[...].astype(jnp.float32))
    loss_o[...] = LN2 * jnp.sum(loss[...], axis=0, keepdims=True)


def text_row(s, h, core):
    return pl.multiple_of(((s * H + h) * 2 + core) * SR, SR)


def body(pic, cap, mat, sc, sh):
    any_spec = pl.BlockSpec(memory_space=pl.ANY)
    vmem = pl.BlockSpec(memory_space=pltpu.VMEM)
    smem = pl.BlockSpec(memory_space=pltpu.SMEM)
    f32, bf16 = jnp.float32, jnp.bfloat16
    dma = pltpu.SemaphoreType.DMA
    parts = pl.pallas_call(
        kernel,
        name="band",
        out_shape=(
            jax.ShapeDtypeStruct((8, B), f32),
            jax.ShapeDtypeStruct((B, D), f32),
            jax.ShapeDtypeStruct((B, D), bf16),
            jax.ShapeDtypeStruct((B, D), f32),
            jax.ShapeDtypeStruct((B, D), bf16),
        ),
        in_specs=[any_spec] * 5,
        out_specs=(vmem, any_spec, any_spec, any_spec, any_spec),
        scratch_shapes=[
            pltpu.SMEM((2, 1), f32),
            pltpu.VMEM((4 * B, D), bf16),
            pltpu.VMEM((TILES * TR, D), bf16),
            pltpu.VMEM((TILES * TR, 4 * B), bf16),
            pltpu.VMEM((4 * B, TILES * TR), bf16),
            pltpu.VMEM((2, 1, B), jnp.int32),
            pltpu.VMEM((4, 8, B), f32),
            pltpu.VMEM((3, 8, B), f32),
            pltpu.VMEM((4 * B, D), f32),
            pltpu.VMEM((TILES * TR, D), f32),
            pltpu.VMEM((TILES * SR, D), f32),
            pltpu.VMEM((2 * B, D), bf16),
            pltpu.VMEM((B, D), bf16),
            pltpu.VMEM((B, D), bf16),
            pltpu.VMEM((B, D), bf16),
            pltpu.VMEM((2 * B, D), bf16),
            pltpu.VMEM((B, D), bf16),
            pltpu.VMEM((B // 2, D), bf16),
            pltpu.VMEM((B // 2, D), bf16),
            pltpu.VMEM((B // 2, D), bf16),
            dma((4 + H,)),
            dma((2, 2)), dma((2, 2)),
            dma((2,)), dma((2,)),
            dma((2, H)), dma((2, H)),
            dma((3, H)), dma((3, H)),
            dma, dma,
            dma((2, 2)), dma((2, 2)),
            dma((2,)), dma((2,)),
            dma((2, H)), dma((2, H)),
            dma((3, H)), dma((3, H)),
            dma((3,)), dma((3,)),
            dma((1 + H,)),
            dma((H // 2,)), dma((H // 2,)),
            dma((H // 2,)), dma((H // 2,)),
            dma((H // 2,)), dma((H // 2,)),
            dma((H // 2,)), dma((H // 2,)),
        ],
        compiler_params=pltpu.CompilerParams(
            collective_id=0, has_side_effects=True, vmem_limit_bytes=56 * 2**20
        ),
        cost_estimate=pl.CostEstimate(flops=7247757312, bytes_accessed=3600000, transcendentals=3145728),
    )(pic, cap.reshape(H, SR, D), mat.reshape(1, B), sc, sh)
    blocks = 2
    rows = pl.BlockSpec((B // blocks, D), lambda i: (i, 0))
    loss, di, dt = pl.pallas_call(
        finish,
        name="finish",
        grid=(blocks,),
        out_shape=(
            jax.ShapeDtypeStruct((1, B), f32),
            jax.ShapeDtypeStruct((B, D), f32),
            jax.ShapeDtypeStruct((B, D), f32),
        ),
        in_specs=[smem, pl.BlockSpec((8, B), lambda i: (0, 0)), rows, rows, rows, rows],
        out_specs=(pl.BlockSpec((1, B), lambda i: (0, 0)), rows, rows),
    )(sc, *parts)
    return loss.reshape(B), di, dt


def solution(mesh):
    return jax.shard_map(
        body,
        mesh=mesh,
        in_specs=(P(("img", "txt"), None), P(("img", "txt"), None), P(("img", "txt")), P(), P()),
        out_specs=(P(("img", "txt")), P(("img", "txt"), None), P(("img", "txt"), None)),
        check_vma=False,
    )
```

```python
import functools

import jax
import jax.numpy as jnp
from jax import lax
from jax.experimental import pallas as pl
from jax.experimental.pallas import tpu as pltpu
from jax.sharding import PartitionSpec as P

MESH = pl.DeviceIdType.MESH
D = 1152
B = 256
HALF = 128
H = 4
SR = B // H
TR = 2 * SR
TILES = 3 * H
NIMG = 64
LOG2E = 1.4426950408889634
LN2 = 0.6931471805599453
SERIES_LIMIT = 2.0**-6


def kernel(
    pic, cap, mat, sc, sh, loss_o, pi_o, rx_late, q0_o, ry_o,
    scal, img, txt, wt, wn, matm, lacc, lrecv, pi, pt, rcc,
    sx_dir, rx_pure, sx_rel, rx_rel, sy_q, ry_q2, tr, tq, rq, lout,
    lsem, ag_s, ag_r, fw_s, fw_r, ty_s, ty_r, tc_s, tc_r, m_s, m_r,
    dir_s, dir_r, rel_s, rel_r, q_s, q_r, ex_s, ex_r, l_s, l_r, o_s,
    tr_s, tr_r, tf_s, tf_r, tq_s, tq_r, tg_s, tg_r,
):
    gi = lax.axis_index("img")
    ti = lax.axis_index("txt")
    row2 = (gi // 2) * 2
    xlo = gi % 2
    xhi = ti // 2
    core = ti % 2
    other = 1 - core
    odd = xlo == 1
    even = xlo == 0

    x_up = (row2 + 1 - xlo, ((xhi + xlo) % 2) * 2 + core)
    x_dn = (row2 + 1 - xlo, ((xhi + 1 - xlo) % 2) * 2 + core)
    x_far = (gi, (1 - xhi) * 2 + core)
    y_up = ((gi + 2) % NIMG, ti)
    y_dn = ((gi + NIMG - 2) % NIMG, ti)
    sib = (gi, xhi * 2 + other)
    y, z = (gi // 2) % 4, gi // 8
    above, below = (y + 1) % 4, (y + 3) % 4

    def at(yy, zz):
        return ((zz + 8) % 8 * 8 + yy * 2 + xlo, ti)

    far_up, far_dn = at(above, z), at(below, z)
    hand_to, hand_from = at(below, z + above // 2), at(above, z - 1 + y // 2)
    home_to, home_from = at(above, z - 1 + below // 2), at(below, z + 1 - ((y + 2) % 4) // 2)

    barrier = pltpu.get_barrier_semaphore()
    partners = (x_up, x_dn, x_far, y_up, y_dn, sib)
    partners += (far_up, far_dn, hand_to, hand_from, home_to, home_from)
    for dev in partners:
        pl.semaphore_signal(barrier, inc=1, device_id=dev, device_id_type=MESH)

    own_img = pltpu.make_async_copy(pic, img.at[pl.ds(0, B)], lsem.at[0])
    own_img.start()
    own_txt = []
    for h in range(H):
        own_txt.append(
            pltpu.make_async_copy(cap.at[h], txt.at[pl.ds(text_row(0, h, core), SR)], lsem.at[1 + h])
        )
        own_txt[h].start()
    small = [
        pltpu.make_async_copy(sc, scal.at[0], lsem.at[1 + H]),
        pltpu.make_async_copy(sh, scal.at[1], lsem.at[2 + H]),
        pltpu.make_async_copy(mat, matm.at[0], lsem.at[3 + H]),
    ]
    for copy in small:
        copy.start()
    lacc[...] = jnp.zeros_like(lacc)
    pl.semaphore_wait(barrier, len(partners))

    def remote(src, dst, s, r, dev):
        return pltpu.make_async_remote_copy(
            src_ref=src, dst_ref=dst, send_sem=s, recv_sem=r, device_id=dev, device_id_type=MESH
        )

    def ag(d, half):
        rows = pl.ds(half * HALF, HALF)
        to_pos = 3 - d
        return remote(
            pic.at[rows], img.at[pl.ds(to_pos * B + half * HALF, HALF)],
            ag_s.at[d, half], ag_r.at[d, half], x_up if d == 0 else x_dn,
        )

    def fw(d):
        return remote(
            img.at[pl.ds((3 - d) * B + d * HALF, HALF)], img.at[pl.ds(B + d * HALF, HALF)],
            fw_s.at[d], fw_r.at[d], x_up if d == 0 else x_dn,
        )

    def ty(s, h):
        dst = txt.at[pl.ds(text_row(s, h, core), SR)]
        src = cap.at[h] if s == 1 else txt.at[pl.ds(text_row(s - 1, h, core), SR)]
        return remote(src, dst, ty_s.at[s - 1, h], ty_r.at[s - 1, h], y_up)

    def tc(s, h, receive=False):
        src = cap.at[h] if s == 0 else txt.at[pl.ds(text_row(s, h, core), SR)]
        dst = txt.at[pl.ds(text_row(s, h, other if receive else core), SR)]
        return remote(src, dst, tc_s.at[s, h], tc_r.at[s, h], sib)

    def there(i):
        return remote(cap.at[H // 2 + i], tr.at[pl.ds(i * SR, SR)], tr_s.at[i], tr_r.at[i], far_dn)

    def onward(i):
        dst = txt.at[pl.ds(text_row(2, H // 2 + i, core), SR)]
        return remote(tr.at[pl.ds(i * SR, SR)], dst, tf_s.at[i], tf_r.at[i], hand_to)

    far_match = remote(mat, matm.at[1], m_s, m_r, x_far)
    far_match.start()
    ty(1, 0).start()
    pl.when(odd)(there(0).start)
    ag(0, 0).start()
    ag(1, 1).start()
    pl.when(odd)(there(1).start)
    for h in range(H):
        tc(0, h).start()
    ty(1, 1).start()
    ag(0, 1).start()
    ag(1, 0).start()
    for h in range(2, H):
        ty(1, h).start()

    for copy in small:
        copy.wait()
    scale = scal[0, 0] * LOG2E
    shift = scal[1, 0] * LOG2E
    text_base = gi * 1024 + xhi * 512

    def scores(tile, count, pos, labelled, has_label=None):
        n = count * TR
        rows = pl.ds(pl.multiple_of(tile * TR, TR), n)
        images = pl.ds(pl.multiple_of(pos * B, B), B)
        sims = lax.dot_general(
            txt[rows, :], img[images, :], (((1,), (1,)), ((), ())), preferred_element_type=jnp.float32
        )
        x = scale * sims + shift
        e = jnp.exp2(-jnp.abs(x))
        u = 1.0 + e
        r = pltpu.reciprocal(u, approx=True)
        big = r * (2.0 - u * r)
        small = e * big
        series = e * (LOG2E - e * (LOG2E / 2 - e * (LOG2E / 3)))
        lp = jnp.where(e < SERIES_LIMIT, series, jnp.log2(u))
        positive = x >= 0.0
        if labelled:
            i = lax.broadcasted_iota(jnp.int32, (n, 1), 0)
            ids = text_base + ((i % TR) // SR) * B + (i // TR) * SR + i % SR
            if has_label is not None:
                ids = jnp.where(has_label, ids, -1)
            label = ids == matm[pos]
            w = jnp.where(jnp.logical_xor(positive, label), big, small)
            w = jnp.where(label, -w, w)
            loss = lp + jnp.maximum(jnp.where(label, -x, x), 0.0)
        else:
            w = jnp.where(positive, big, small)
            loss = lp + jnp.maximum(x, 0.0)
        w = w.astype(jnp.bfloat16)
        wt[rows, images] = w
        wn[images, rows] = w.T
        lacc[pos] += jnp.sum(loss.reshape(n // 8, 8, B), axis=0)

    def scores_loop(n, tile_of, count, pos_of):
        @pl.loop(0, n)
        def _(j):
            scores(tile_of(j), count, pos_of(j), False)

    def own_scores(pos):
        scores(0, H, pos, True)

    def far_scores():
        @pl.loop(0, 2)
        def _(j):
            scores(j * H, H, 1, True, j == 0)

    def image_part(pos, tile, count):
        cols = pl.ds(tile * TR, count * TR)
        pi[pl.ds(pos * B, B)] = jnp.dot(
            wn[pl.ds(pos * B, B), cols], txt[cols, :], preferred_element_type=jnp.float32
        )

    def text_part(s, h, count, first=0, blocks=4):
        rows = pl.ds((s * H + h) * TR, count * TR)
        ks = pl.ds(first * B, blocks * B)
        pt[rows] = jnp.dot(wt[rows, ks], img[ks, :], preferred_element_type=jnp.float32)
        for k in range(h, h + count):
            ex(s, k).start()

    def ex(s, h):
        tile = s * H + h
        return remote(
            pt.at[pl.ds(text_row(s, h, other), SR)], rcc.at[pl.ds(tile * SR, SR)],
            ex_s.at[s, h], ex_r.at[s, h], sib,
        )

    def chip_sum(s, h):
        tile = s * H + h
        ex(s, h).wait_recv()
        return pt[pl.ds(text_row(s, h, core), SR), :] + rcc[pl.ds(tile * SR, SR), :]

    def q(s, h):
        rows = pl.ds(h * SR, SR)
        dst = ry_o if s == 1 else ry_q2
        return remote(
            sy_q.at[pl.ds(((s - 1) * H + h) * SR, SR)], dst.at[rows], q_s.at[s - 1, h], q_r.at[s - 1, h], y_dn
        )

    def q_send(s, h, chain=False):
        value = chip_sum(s, h)
        if chain:
            q(2, h).wait_recv()
            value = value + ry_q2[pl.ds(h * SR, SR), :].astype(jnp.float32)
        sy_q[pl.ds(((s - 1) * H + h) * SR, SR), :] = value.astype(jnp.bfloat16)
        q(s, h).start()

    def back(h):
        rows = pl.ds(h * SR, SR)
        return remote(sy_q.at[pl.ds((H + h) * SR, SR)], tq.at[rows], tq_s.at[h], tq_r.at[h], far_up)

    def home(h):
        rows = pl.ds(h * SR, SR)
        return remote(tq.at[rows], rq.at[rows], tg_s.at[h], tg_r.at[h], home_to)

    def back_send(h):
        sy_q[pl.ds((H + h) * SR, SR), :] = chip_sum(2, h).astype(jnp.bfloat16)
        back(h).start()

    def home_send(h):
        back(h).wait_recv()
        home(h).start()

    def rel(d):
        rows = pl.ds(d * HALF, HALF)
        return remote(
            sx_rel.at[rows], rx_rel.at[rows], rel_s.at[d], rel_r.at[d], x_up if d == 0 else x_dn
        )

    def rel_send():
        sx_rel[...] = pi[pl.ds(B, B), :].astype(jnp.bfloat16)
        rel(0).start()
        rel(1).start()

    def direct(d, half):
        rows = pl.ds(half * HALF, HALF)
        return remote(
            sx_dir.at[pl.ds(d * B + half * HALF, HALF)], (rx_late if d == half else rx_pure).at[rows],
            dir_s.at[d, half], dir_r.at[d, half], x_up if d == 0 else x_dn,
        )

    def direct_send(d, relayed):
        half = d if relayed else 1 - d
        value = pi[pl.ds((2 + d) * B + half * HALF, HALF), :]
        if relayed:
            rel(d).wait_recv()
            value = value + rx_rel[pl.ds(d * HALF, HALF), :].astype(jnp.float32)
        sx_dir[pl.ds(d * B + half * HALF, HALF), :] = value.astype(jnp.bfloat16)
        direct(d, half).start()

    def loss_copy(pos):
        dev = {1: x_far, 2: x_up, 3: x_dn}[pos]
        return remote(lacc.at[pos], lrecv.at[pos - 1], l_s.at[pos - 1], l_r.at[pos - 1], dev)

    def arrive(s, h):
        (onward(h - H // 2) if s == 2 and h >= H // 2 else ty(s, h)).wait_recv()
        tc(s, h).start()

    def arrive_sib(s, h):
        tc(s, h, receive=True).wait_recv()

    def pass_on(h):
        there(h).wait_recv()
        onward(h).start()

    def hand_on_images():
        for d in range(2):
            ag(d, d).wait_recv()
            fw(d).start()

    def neighbours():
        for d in range(2):
            ag(d, 1 - d).wait_recv()

    def far():
        fw(0).wait_recv()
        fw(1).wait_recv()

    own_img.wait()
    for h in range(H):
        own_txt[h].wait()
    for h in range(H):
        tc(0, h, receive=True).wait_recv()
    far_match.wait_recv()
    own_scores(0)

    @pl.when(even)
    def _():
        arrive(1, 0)
        arrive(1, 1)
        hand_on_images()
        arrive_sib(1, 0)
        arrive_sib(1, 1)
        scores_loop(1, lambda j: H + j, 2, lambda j: 0)
        arrive(1, 2)
        neighbours()
        arrive(1, 3)
        scores_loop(2, lambda j: 0, H, lambda j: 2 + j)
        arrive_sib(1, 2)
        arrive_sib(1, 3)
        scores_loop(2, lambda j: H, H, lambda j: 2 + j)
        image_part(2, 0, 2 * H)
        direct_send(0, False)
        image_part(3, 0, 2 * H)
        direct_send(1, False)
        scores_loop(1, lambda j: H + 2 + j, 2, lambda j: 0)
        far()
        far_scores()
        image_part(1, 0, 2 * H)
        rel_send()
        text_part(1, 0, 2)
        for pos in (1, 2, 3):
            loss_copy(pos).start()
        text_part(1, 2, 2)
        q_send(1, 0)
        q_send(1, 1)
        text_part(0, 0, 2)
        q_send(1, 2)
        q_send(1, 3)
        text_part(0, 2, 2)
        image_part(0, 0, 2 * H)
        direct_send(0, True)
        direct_send(1, True)

    @pl.when(odd)
    def _():
        arrive(1, 0)
        ty(2, 0).start()
        arrive(1, 1)
        ty(2, 1).start()
        hand_on_images()
        arrive_sib(1, 0)
        arrive_sib(1, 1)
        scores_loop(1, lambda j: H + j, 2, lambda j: 0)
        pass_on(0)
        arrive(1, 2)
        pass_on(1)
        arrive(2, 2)
        neighbours()
        arrive(1, 3)
        scores_loop(2, lambda j: H, 2, lambda j: 2 + j)
        arrive_sib(1, 2)
        arrive_sib(1, 3)
        scores_loop(3, lambda j: H + 2, 2, lambda j: j + jnp.minimum(j, 1))
        arrive(2, 3)
        arrive(2, 0)
        arrive_sib(2, 2)
        scores_loop(2, lambda j: 2 * H + 2, 1, lambda j: 2 + j)
        text_part(2, 2, 1, 2, 2)
        far()
        far_scores()
        q_send(2, 2)
        arrive(2, 1)
        image_part(1, 0, 2 * H)
        rel_send()
        text_part(1, 0, 2)
        arrive_sib(2, 0)
        arrive_sib(2, 1)
        scores_loop(2, lambda j: 2 * H, 2, lambda j: 2 + j)
        q_send(1, 0)
        text_part(2, 0, 2, 2, 2)
        q_send(1, 1)
        arrive_sib(2, 3)
        scores_loop(2, lambda j: 2 * H + 3, 1, lambda j: 2 + j)
        back_send(0)
        back_send(1)
        image_part(2, H, 2 * H)
        direct_send(0, False)
        image_part(3, H, 2 * H)
        direct_send(1, False)
        text_part(2, 3, 1, 2, 2)
        text_part(1, 2, 2)
        q_send(2, 3)
        for pos in (1, 2, 3):
            loss_copy(pos).start()
        image_part(0, 0, 2 * H)
        text_part(0, 0, 2, 0, 2)
        text_part(0, 2, 2, 0, 2)
        q_send(1, 2, chain=True)
        home_send(0)
        direct_send(0, True)
        direct_send(1, True)
        q_send(1, 3, chain=True)
        home_send(1)

    for pos in (1, 2, 3):
        loss_copy(pos).wait_recv()
    lout[pl.ds(0, 8), :] = lacc[0] + lrecv[0] + lrecv[1] + lrecv[2]
    lout[pl.ds(8, 8), :] = jnp.full((8, B), scal[0, 0], jnp.float32)
    loss_out = pltpu.make_async_copy(lout, loss_o, o_s.at[1 + H])
    loss_out.start()

    def q0_out(h):
        rows = pl.ds(text_row(0, h, core), SR)
        return pltpu.make_async_copy(pt.at[rows], q0_o.at[pl.ds(h * SR, SR)], o_s.at[1 + h])

    for h in range(H // 2, H):
        pt[pl.ds(text_row(0, h, core), SR), :] = chip_sum(0, h)
        q0_out(h).start()
    direct(0, 1).wait_recv()
    direct(1, 0).wait_recv()
    pi[pl.ds(0, B), :] += rx_pure[...].astype(jnp.float32)
    pi_out = pltpu.make_async_copy(pi.at[pl.ds(0, B)], pi_o, o_s.at[0])
    pi_out.start()
    for h in range(H // 2):
        rows = pl.ds(text_row(0, h, core), SR)
        pt[rows, :] = chip_sum(0, h)

        @pl.when(odd)
        def _():
            home(h).wait_recv()
            pt[rows, :] += rq[pl.ds(h * SR, SR), :].astype(jnp.float32)

        q0_out(h).start()

    for d in range(2):
        fw(d).wait_send()
        rel(d).wait_send()
        for half in range(2):
            ag(d, half).wait_send()
    for h in range(H):
        ty(1, h).wait_send()
        tc(0, h).wait_send()
        tc(1, h).wait_send()
        ex(0, h).wait_send()
        ex(1, h).wait_send()
    far_match.wait_send()
    for pos in (1, 2, 3):
        loss_copy(pos).wait_send()

    @pl.when(odd)
    def _():
        for h in range(H):
            tc(2, h).wait_send()
            ex(2, h).wait_send()
        for h in range(H // 2):
            ty(2, h).wait_send()
            there(h).wait_send()
            onward(h).wait_send()
            q(2, H // 2 + h).wait_send()
            back(h).wait_send()
            home(h).wait_send()

    for h in range(H):
        q0_out(h).wait()
    pi_out.wait()
    loss_out.wait()
    for d in range(2):
        for half in range(2):
            direct(d, half).wait_send()
        direct(d, d).wait_recv()
    for h in range(H):
        q(1, h).wait()


def finish(loss, pi, late, q0, ry, loss_o, di_o, dt_o):
    s = loss[8:9, 0:1]
    di_o[...] = s * (pi[...] + late[...].astype(jnp.float32))
    dt_o[...] = s * (q0[...] + ry[...].astype(jnp.float32))
    loss_o[...] = LN2 * jnp.sum(loss[0:8, :], axis=0, keepdims=True)


def text_row(s, h, core):
    return pl.multiple_of(((s * H + h) * 2 + core) * SR, SR)


def body(pic, cap, mat, sc, sh):
    any_spec = pl.BlockSpec(memory_space=pl.ANY)
    hbm = pl.BlockSpec(memory_space=pltpu.HBM)
    f32, bf16 = jnp.float32, jnp.bfloat16
    dma = pltpu.SemaphoreType.DMA
    parts = pl.pallas_call(
        kernel,
        name="band",
        out_shape=(
            jax.ShapeDtypeStruct((16, B), f32),
            jax.ShapeDtypeStruct((B, D), f32),
            jax.ShapeDtypeStruct((B, D), bf16),
            jax.ShapeDtypeStruct((B, D), f32),
            jax.ShapeDtypeStruct((B, D), bf16),
        ),
        in_specs=[any_spec] * 3 + [hbm] * 2,
        out_specs=(any_spec,) * 5,
        scratch_shapes=[
            pltpu.SMEM((2, 1), f32),
            pltpu.VMEM((4 * B, D), bf16),
            pltpu.VMEM((TILES * TR, D), bf16),
            pltpu.VMEM((TILES * TR, 4 * B), bf16),
            pltpu.VMEM((4 * B, TILES * TR), bf16),
            pltpu.VMEM((2, 1, B), jnp.int32),
            pltpu.VMEM((4, 8, B), f32),
            pltpu.VMEM((3, 8, B), f32),
            pltpu.VMEM((4 * B, D), f32),
            pltpu.VMEM((TILES * TR, D), f32),
            pltpu.VMEM((TILES * SR, D), f32),
            pltpu.VMEM((2 * B, D), bf16),
            pltpu.VMEM((B, D), bf16),
            pltpu.VMEM((B, D), bf16),
            pltpu.VMEM((B, D), bf16),
            pltpu.VMEM((2 * B, D), bf16),
            pltpu.VMEM((B, D), bf16),
            pltpu.VMEM((B // 2, D), bf16),
            pltpu.VMEM((B // 2, D), bf16),
            pltpu.VMEM((B // 2, D), bf16),
            pltpu.VMEM((16, B), f32),
            dma((4 + H,)),
            dma((2, 2)), dma((2, 2)),
            dma((2,)), dma((2,)),
            dma((2, H)), dma((2, H)),
            dma((3, H)), dma((3, H)),
            dma, dma,
            dma((2, 2)), dma((2, 2)),
            dma((2,)), dma((2,)),
            dma((2, H)), dma((2, H)),
            dma((3, H)), dma((3, H)),
            dma((3,)), dma((3,)),
            dma((2 + H,)),
            dma((H // 2,)), dma((H // 2,)),
            dma((H // 2,)), dma((H // 2,)),
            dma((H // 2,)), dma((H // 2,)),
            dma((H // 2,)), dma((H // 2,)),
        ],
        compiler_params=pltpu.CompilerParams(
            collective_id=0, has_side_effects=True, vmem_limit_bytes=56 * 2**20
        ),
        cost_estimate=pl.CostEstimate(flops=7247757312, bytes_accessed=3600000, transcendentals=3145728),
    )(pic, cap.reshape(H, SR, D), mat.reshape(1, B), sc, sh)
    blocks = 2
    rows = pl.BlockSpec((B // blocks, D), lambda i: (i, 0))
    loss, di, dt = pl.pallas_call(
        finish,
        name="finish",
        grid=(blocks,),
        out_shape=(
            jax.ShapeDtypeStruct((1, B), f32),
            jax.ShapeDtypeStruct((B, D), f32),
            jax.ShapeDtypeStruct((B, D), f32),
        ),
        in_specs=[pl.BlockSpec((16, B), lambda i: (0, 0)), rows, rows, rows, rows],
        out_specs=(pl.BlockSpec((1, B), lambda i: (0, 0)), rows, rows),
    )(*parts)
    return loss.reshape(B), di, dt


def solution(mesh):
    return jax.shard_map(
        body,
        mesh=mesh,
        in_specs=(P(("img", "txt"), None), P(("img", "txt"), None), P(("img", "txt")), P(), P()),
        out_specs=(P(("img", "txt")), P(("img", "txt"), None), P(("img", "txt"), None)),
        check_vma=False,
    )
```

```python
import functools

import jax
import jax.numpy as jnp
from jax import lax
from jax.experimental import pallas as pl
from jax.experimental.pallas import tpu as pltpu
from jax.sharding import PartitionSpec as P

MESH = pl.DeviceIdType.MESH
D = 1152
B = 256
HALF = 128
H = 4
SR = B // H
TR = 2 * SR
TILES = 3 * H
NIMG = 64
LOG2E = 1.4426950408889634
LN2 = 0.6931471805599453
SERIES_LIMIT = 2.0**-6


def kernel(
    pic, cap, mat, sc, sh, loss_o, pi_o, rx_late, q0_o, ry_o,
    scal, img, txt, wt, wn, matm, lacc, lrecv, pi, pt, rcc,
    sx_dir, rx_pure, sx_rel, rx_rel, sy_q, ry_q2, tr, tq, rq, lout,
    lsem, ag_s, ag_r, fw_s, fw_r, ty_s, ty_r, tc_s, tc_r, m_s, m_r,
    dir_s, dir_r, rel_s, rel_r, q_s, q_r, ex_s, ex_r, l_s, l_r, o_s,
    tr_s, tr_r, tf_s, tf_r, tq_s, tq_r, tg_s, tg_r,
):
    gi = lax.axis_index("img")
    ti = lax.axis_index("txt")
    row2 = (gi // 2) * 2
    xlo = gi % 2
    xhi = ti // 2
    core = ti % 2
    other = 1 - core
    odd = xlo == 1
    even = xlo == 0

    x_up = (row2 + 1 - xlo, ((xhi + xlo) % 2) * 2 + core)
    x_dn = (row2 + 1 - xlo, ((xhi + 1 - xlo) % 2) * 2 + core)
    x_far = (gi, (1 - xhi) * 2 + core)
    y_up = ((gi + 2) % NIMG, ti)
    y_dn = ((gi + NIMG - 2) % NIMG, ti)
    sib = (gi, xhi * 2 + other)
    y, z = (gi // 2) % 4, gi // 8
    above, below = (y + 1) % 4, (y + 3) % 4

    def at(yy, zz):
        return ((zz + 8) % 8 * 8 + yy * 2 + xlo, ti)

    far_up, far_dn = at(above, z), at(below, z)
    hand_to, hand_from = at(below, z + above // 2), at(above, z - 1 + y // 2)
    home_to, home_from = at(above, z - 1 + below // 2), at(below, z + 1 - ((y + 2) % 4) // 2)

    barrier = pltpu.get_barrier_semaphore()
    partners = (x_up, x_dn, x_far, y_up, y_dn, sib)
    partners += (far_up, far_dn, hand_to, hand_from, home_to, home_from)
    for dev in partners:
        pl.semaphore_signal(barrier, inc=1, device_id=dev, device_id_type=MESH)

    own_img = pltpu.make_async_copy(pic, img.at[pl.ds(0, B)], lsem.at[0])
    own_img.start()
    own_txt = []
    for h in range(H):
        own_txt.append(
            pltpu.make_async_copy(cap.at[h], txt.at[pl.ds(text_row(0, h, core), SR)], lsem.at[1 + h])
        )
        own_txt[h].start()
    small = [
        pltpu.make_async_copy(sc, scal.at[0], lsem.at[1 + H]),
        pltpu.make_async_copy(sh, scal.at[1], lsem.at[2 + H]),
        pltpu.make_async_copy(mat, matm.at[0], lsem.at[3 + H]),
    ]
    for copy in small:
        copy.start()
    lacc[...] = jnp.zeros_like(lacc)
    pl.semaphore_wait(barrier, len(partners))

    def remote(src, dst, s, r, dev):
        return pltpu.make_async_remote_copy(
            src_ref=src, dst_ref=dst, send_sem=s, recv_sem=r, device_id=dev, device_id_type=MESH
        )

    def ag(d, half):
        rows = pl.ds(half * HALF, HALF)
        to_pos = 3 - d
        return remote(
            pic.at[rows], img.at[pl.ds(to_pos * B + half * HALF, HALF)],
            ag_s.at[d, half], ag_r.at[d, half], x_up if d == 0 else x_dn,
        )

    def fw(d):
        return remote(
            img.at[pl.ds((3 - d) * B + d * HALF, HALF)], img.at[pl.ds(B + d * HALF, HALF)],
            fw_s.at[d], fw_r.at[d], x_up if d == 0 else x_dn,
        )

    def ty(s, h):
        dst = txt.at[pl.ds(text_row(s, h, core), SR)]
        src = cap.at[h] if s == 1 else txt.at[pl.ds(text_row(s - 1, h, core), SR)]
        return remote(src, dst, ty_s.at[s - 1, h], ty_r.at[s - 1, h], y_up)

    def tc(s, h, receive=False):
        src = cap.at[h] if s == 0 else txt.at[pl.ds(text_row(s, h, core), SR)]
        dst = txt.at[pl.ds(text_row(s, h, other if receive else core), SR)]
        return remote(src, dst, tc_s.at[s, h], tc_r.at[s, h], sib)

    def there(i):
        return remote(cap.at[H // 2 + i], tr.at[pl.ds(i * SR, SR)], tr_s.at[i], tr_r.at[i], far_dn)

    def onward(i):
        dst = txt.at[pl.ds(text_row(2, H // 2 + i, core), SR)]
        return remote(tr.at[pl.ds(i * SR, SR)], dst, tf_s.at[i], tf_r.at[i], hand_to)

    far_match = remote(mat, matm.at[1], m_s, m_r, x_far)
    far_match.start()
    ty(1, 0).start()
    pl.when(odd)(there(0).start)
    ag(0, 0).start()
    ag(1, 1).start()
    pl.when(odd)(there(1).start)
    for h in range(H):
        tc(0, h).start()
    ty(1, 1).start()
    ag(0, 1).start()
    ag(1, 0).start()
    for h in range(2, H):
        ty(1, h).start()

    for copy in small:
        copy.wait()
    scale = scal[0, 0] * LOG2E
    shift = scal[1, 0] * LOG2E
    text_base = gi * 1024 + xhi * 512

    def scores(tile, count, pos, labelled, has_label=None):
        n = count * TR
        rows = pl.ds(pl.multiple_of(tile * TR, TR), n)
        images = pl.ds(pl.multiple_of(pos * B, B), B)
        sims = lax.dot_general(
            txt[rows, :], img[images, :], (((1,), (1,)), ((), ())), preferred_element_type=jnp.float32
        )
        x = scale * sims + shift
        e = jnp.exp2(-jnp.abs(x))
        u = 1.0 + e
        r = pltpu.reciprocal(u, approx=True)
        big = r * (2.0 - u * r)
        small = e * big
        series = e * (LOG2E - e * (LOG2E / 2 - e * (LOG2E / 3)))
        lp = jnp.where(e < SERIES_LIMIT, series, jnp.log2(u))
        positive = x >= 0.0
        if labelled:
            i = lax.broadcasted_iota(jnp.int32, (n, 1), 0)
            ids = text_base + ((i % TR) // SR) * B + (i // TR) * SR + i % SR
            if has_label is not None:
                ids = jnp.where(has_label, ids, -1)
            label = ids == matm[pos]
            w = jnp.where(jnp.logical_xor(positive, label), big, small)
            w = jnp.where(label, -w, w)
            loss = lp + jnp.maximum(jnp.where(label, -x, x), 0.0)
        else:
            w = jnp.where(positive, big, small)
            loss = lp + jnp.maximum(x, 0.0)
        w = w.astype(jnp.bfloat16)
        wt[rows, images] = w
        wn[images, rows] = w.T
        lacc[pos] += jnp.sum(loss.reshape(n // 8, 8, B), axis=0)

    def scores_loop(n, tile_of, count, pos_of):
        @pl.loop(0, n)
        def _(j):
            scores(tile_of(j), count, pos_of(j), False)

    def own_scores(pos):
        scores(0, H, pos, True)

    def far_scores():
        @pl.loop(0, 2)
        def _(j):
            scores(j * H, H, 1, True, j == 0)

    def image_part(pos, tile, count):
        cols = pl.ds(tile * TR, count * TR)
        pi[pl.ds(pos * B, B)] = jnp.dot(
            wn[pl.ds(pos * B, B), cols], txt[cols, :], preferred_element_type=jnp.float32
        )

    def text_part(s, h, count, first=0, blocks=4):
        rows = pl.ds((s * H + h) * TR, count * TR)
        ks = pl.ds(first * B, blocks * B)
        pt[rows] = jnp.dot(wt[rows, ks], img[ks, :], preferred_element_type=jnp.float32)
        for k in range(h, h + count):
            ex(s, k).start()

    def ex(s, h):
        tile = s * H + h
        return remote(
            pt.at[pl.ds(text_row(s, h, other), SR)], rcc.at[pl.ds(tile * SR, SR)],
            ex_s.at[s, h], ex_r.at[s, h], sib,
        )

    def chip_sum(s, h):
        tile = s * H + h
        ex(s, h).wait_recv()
        return pt[pl.ds(text_row(s, h, core), SR), :] + rcc[pl.ds(tile * SR, SR), :]

    def q(s, h):
        rows = pl.ds(h * SR, SR)
        dst = ry_o if s == 1 else ry_q2
        return remote(
            sy_q.at[pl.ds(((s - 1) * H + h) * SR, SR)], dst.at[rows], q_s.at[s - 1, h], q_r.at[s - 1, h], y_dn
        )

    def q_send(s, h, chain=False):
        value = chip_sum(s, h)
        if chain:
            q(2, h).wait_recv()
            value = value + ry_q2[pl.ds(h * SR, SR), :].astype(jnp.float32)
        sy_q[pl.ds(((s - 1) * H + h) * SR, SR), :] = value.astype(jnp.bfloat16)
        q(s, h).start()

    def back(h):
        rows = pl.ds(h * SR, SR)
        return remote(sy_q.at[pl.ds((H + h) * SR, SR)], tq.at[rows], tq_s.at[h], tq_r.at[h], far_up)

    def home(h):
        rows = pl.ds(h * SR, SR)
        return remote(tq.at[rows], rq.at[rows], tg_s.at[h], tg_r.at[h], home_to)

    def back_send(h):
        sy_q[pl.ds((H + h) * SR, SR), :] = chip_sum(2, h).astype(jnp.bfloat16)
        back(h).start()

    def home_send(h):
        back(h).wait_recv()
        home(h).start()

    def rel(d):
        rows = pl.ds(d * HALF, HALF)
        return remote(
            sx_rel.at[rows], rx_rel.at[rows], rel_s.at[d], rel_r.at[d], x_up if d == 0 else x_dn
        )

    def rel_send():
        sx_rel[...] = pi[pl.ds(B, B), :].astype(jnp.bfloat16)
        rel(0).start()
        rel(1).start()

    def direct(d, half):
        rows = pl.ds(half * HALF, HALF)
        return remote(
            sx_dir.at[pl.ds(d * B + half * HALF, HALF)], (rx_late if d == half else rx_pure).at[rows],
            dir_s.at[d, half], dir_r.at[d, half], x_up if d == 0 else x_dn,
        )

    def direct_send(d, relayed):
        half = d if relayed else 1 - d
        value = pi[pl.ds((2 + d) * B + half * HALF, HALF), :]
        if relayed:
            rel(d).wait_recv()
            value = value + rx_rel[pl.ds(d * HALF, HALF), :].astype(jnp.float32)
        sx_dir[pl.ds(d * B + half * HALF, HALF), :] = value.astype(jnp.bfloat16)
        direct(d, half).start()

    def loss_copy(pos):
        dev = {1: x_far, 2: x_up, 3: x_dn}[pos]
        return remote(lacc.at[pos], lrecv.at[pos - 1], l_s.at[pos - 1], l_r.at[pos - 1], dev)

    def arrive(s, h):
        (onward(h - H // 2) if s == 2 and h >= H // 2 else ty(s, h)).wait_recv()
        tc(s, h).start()

    def arrive_sib(s, h):
        tc(s, h, receive=True).wait_recv()

    def pass_on(h):
        there(h).wait_recv()
        onward(h).start()

    def hand_on_images():
        for d in range(2):
            ag(d, d).wait_recv()
            fw(d).start()

    def neighbours():
        for d in range(2):
            ag(d, 1 - d).wait_recv()

    def far():
        fw(0).wait_recv()
        fw(1).wait_recv()

    own_img.wait()
    for h in range(H):
        own_txt[h].wait()
    for h in range(H):
        tc(0, h, receive=True).wait_recv()
    far_match.wait_recv()
    own_scores(0)

    @pl.when(even)
    def _():
        arrive(1, 0)
        arrive(1, 1)
        hand_on_images()
        arrive_sib(1, 0)
        arrive_sib(1, 1)
        scores_loop(1, lambda j: H + j, 2, lambda j: 0)
        arrive(1, 2)
        neighbours()
        arrive(1, 3)
        scores_loop(2, lambda j: 0, H, lambda j: 2 + j)
        arrive_sib(1, 2)
        arrive_sib(1, 3)
        scores_loop(2, lambda j: H, H, lambda j: 2 + j)
        image_part(2, 0, 2 * H)
        image_part(3, 0, 2 * H)
        scores_loop(1, lambda j: H + 2 + j, 2, lambda j: 0)
        far()
        far_scores()
        image_part(1, 0, 2 * H)
        rel_send()
        direct_send(0, False)
        direct_send(1, False)
        text_part(1, 0, 2)
        for pos in (1, 2, 3):
            loss_copy(pos).start()
        text_part(1, 2, 2)
        q_send(1, 0)
        q_send(1, 1)
        text_part(0, 0, 2)
        q_send(1, 2)
        q_send(1, 3)
        text_part(0, 2, 2)
        image_part(0, 0, 2 * H)
        direct_send(0, True)
        direct_send(1, True)

    @pl.when(odd)
    def _():
        arrive(1, 0)
        ty(2, 0).start()
        arrive(1, 1)
        ty(2, 1).start()
        hand_on_images()
        arrive_sib(1, 0)
        arrive_sib(1, 1)
        scores_loop(1, lambda j: H + j, 2, lambda j: 0)
        pass_on(0)
        arrive(1, 2)
        pass_on(1)
        arrive(2, 2)
        neighbours()
        arrive(1, 3)
        scores_loop(2, lambda j: H, 2, lambda j: 2 + j)
        arrive_sib(1, 2)
        arrive_sib(1, 3)
        scores_loop(3, lambda j: H + 2, 2, lambda j: j + jnp.minimum(j, 1))
        arrive(2, 3)
        arrive(2, 0)
        arrive_sib(2, 2)
        scores_loop(2, lambda j: 2 * H + 2, 1, lambda j: 2 + j)
        text_part(2, 2, 1, 2, 2)
        far()
        far_scores()
        q_send(2, 2)
        arrive(2, 1)
        image_part(1, 0, 2 * H)
        rel_send()
        arrive_sib(2, 0)
        arrive_sib(2, 1)
        scores_loop(2, lambda j: 2 * H, 2, lambda j: 2 + j)
        text_part(2, 0, 2, 2, 2)
        text_part(1, 0, 2)
        back_send(0)
        back_send(1)
        arrive_sib(2, 3)
        scores_loop(2, lambda j: 2 * H + 3, 1, lambda j: 2 + j)
        q_send(1, 0)
        q_send(1, 1)
        image_part(2, H, 2 * H)
        direct_send(0, False)
        image_part(3, H, 2 * H)
        direct_send(1, False)
        text_part(2, 3, 1, 2, 2)
        text_part(1, 2, 2)
        q_send(2, 3)
        for pos in (1, 2, 3):
            loss_copy(pos).start()
        image_part(0, 0, 2 * H)
        text_part(0, 0, 2, 0, 2)
        text_part(0, 2, 2, 0, 2)
        q_send(1, 2, chain=True)
        home_send(0)
        direct_send(0, True)
        direct_send(1, True)
        q_send(1, 3, chain=True)
        home_send(1)

    for pos in (1, 2, 3):
        loss_copy(pos).wait_recv()
    lout[pl.ds(0, 8), :] = lacc[0] + lrecv[0] + lrecv[1] + lrecv[2]
    lout[pl.ds(8, 8), :] = jnp.full((8, B), scal[0, 0], jnp.float32)
    loss_out = pltpu.make_async_copy(lout, loss_o, o_s.at[1 + H])
    loss_out.start()

    def q0_out(h):
        rows = pl.ds(text_row(0, h, core), SR)
        return pltpu.make_async_copy(pt.at[rows], q0_o.at[pl.ds(h * SR, SR)], o_s.at[1 + h])

    for h in range(H // 2, H):
        pt[pl.ds(text_row(0, h, core), SR), :] = chip_sum(0, h)
        q0_out(h).start()
    direct(0, 1).wait_recv()
    direct(1, 0).wait_recv()
    pi[pl.ds(0, B), :] += rx_pure[...].astype(jnp.float32)
    pi_out = pltpu.make_async_copy(pi.at[pl.ds(0, B)], pi_o, o_s.at[0])
    pi_out.start()
    for h in range(H // 2):
        rows = pl.ds(text_row(0, h, core), SR)
        pt[rows, :] = chip_sum(0, h)

        @pl.when(odd)
        def _():
            home(h).wait_recv()
            pt[rows, :] += rq[pl.ds(h * SR, SR), :].astype(jnp.float32)

        q0_out(h).start()

    for d in range(2):
        fw(d).wait_send()
        rel(d).wait_send()
        for half in range(2):
            ag(d, half).wait_send()
    for h in range(H):
        ty(1, h).wait_send()
        tc(0, h).wait_send()
        tc(1, h).wait_send()
        ex(0, h).wait_send()
        ex(1, h).wait_send()
    far_match.wait_send()
    for pos in (1, 2, 3):
        loss_copy(pos).wait_send()

    @pl.when(odd)
    def _():
        for h in range(H):
            tc(2, h).wait_send()
            ex(2, h).wait_send()
        for h in range(H // 2):
            ty(2, h).wait_send()
            there(h).wait_send()
            onward(h).wait_send()
            q(2, H // 2 + h).wait_send()
            back(h).wait_send()
            home(h).wait_send()

    for h in range(H):
        q0_out(h).wait()
    pi_out.wait()
    loss_out.wait()
    for d in range(2):
        for half in range(2):
            direct(d, half).wait_send()
        direct(d, d).wait_recv()
    for h in range(H):
        q(1, h).wait()


def finish(loss, pi, late, q0, ry, loss_o, di_o, dt_o):
    s = loss[8:9, 0:1]
    di_o[...] = s * (pi[...] + late[...].astype(jnp.float32))
    dt_o[...] = s * (q0[...] + ry[...].astype(jnp.float32))
    loss_o[...] = LN2 * jnp.sum(loss[0:8, :], axis=0, keepdims=True)


def text_row(s, h, core):
    return pl.multiple_of(((s * H + h) * 2 + core) * SR, SR)


def body(pic, cap, mat, sc, sh):
    any_spec = pl.BlockSpec(memory_space=pl.ANY)
    hbm = pl.BlockSpec(memory_space=pltpu.HBM)
    f32, bf16 = jnp.float32, jnp.bfloat16
    dma = pltpu.SemaphoreType.DMA
    parts = pl.pallas_call(
        kernel,
        name="band",
        out_shape=(
            jax.ShapeDtypeStruct((16, B), f32),
            jax.ShapeDtypeStruct((B, D), f32),
            jax.ShapeDtypeStruct((B, D), bf16),
            jax.ShapeDtypeStruct((B, D), f32),
            jax.ShapeDtypeStruct((B, D), bf16),
        ),
        in_specs=[any_spec] * 3 + [hbm] * 2,
        out_specs=(any_spec,) * 5,
        scratch_shapes=[
            pltpu.SMEM((2, 1), f32),
            pltpu.VMEM((4 * B, D), bf16),
            pltpu.VMEM((TILES * TR, D), bf16),
            pltpu.VMEM((TILES * TR, 4 * B), bf16),
            pltpu.VMEM((4 * B, TILES * TR), bf16),
            pltpu.VMEM((2, 1, B), jnp.int32),
            pltpu.VMEM((4, 8, B), f32),
            pltpu.VMEM((3, 8, B), f32),
            pltpu.VMEM((4 * B, D), f32),
            pltpu.VMEM((TILES * TR, D), f32),
            pltpu.VMEM((TILES * SR, D), f32),
            pltpu.VMEM((2 * B, D), bf16),
            pltpu.VMEM((B, D), bf16),
            pltpu.VMEM((B, D), bf16),
            pltpu.VMEM((B, D), bf16),
            pltpu.VMEM((2 * B, D), bf16),
            pltpu.VMEM((B, D), bf16),
            pltpu.VMEM((B // 2, D), bf16),
            pltpu.VMEM((B // 2, D), bf16),
            pltpu.VMEM((B // 2, D), bf16),
            pltpu.VMEM((16, B), f32),
            dma((4 + H,)),
            dma((2, 2)), dma((2, 2)),
            dma((2,)), dma((2,)),
            dma((2, H)), dma((2, H)),
            dma((3, H)), dma((3, H)),
            dma, dma,
            dma((2, 2)), dma((2, 2)),
            dma((2,)), dma((2,)),
            dma((2, H)), dma((2, H)),
            dma((3, H)), dma((3, H)),
            dma((3,)), dma((3,)),
            dma((2 + H,)),
            dma((H // 2,)), dma((H // 2,)),
            dma((H // 2,)), dma((H // 2,)),
            dma((H // 2,)), dma((H // 2,)),
            dma((H // 2,)), dma((H // 2,)),
        ],
        compiler_params=pltpu.CompilerParams(
            collective_id=0, has_side_effects=True, vmem_limit_bytes=56 * 2**20
        ),
        cost_estimate=pl.CostEstimate(flops=7247757312, bytes_accessed=3600000, transcendentals=3145728),
    )(pic, cap.reshape(H, SR, D), mat.reshape(1, B), sc, sh)
    blocks = 2
    rows = pl.BlockSpec((B // blocks, D), lambda i: (i, 0))
    loss, di, dt = pl.pallas_call(
        finish,
        name="finish",
        grid=(blocks,),
        out_shape=(
            jax.ShapeDtypeStruct((1, B), f32),
            jax.ShapeDtypeStruct((B, D), f32),
            jax.ShapeDtypeStruct((B, D), f32),
        ),
        in_specs=[pl.BlockSpec((16, B), lambda i: (0, 0)), rows, rows, rows, rows],
        out_specs=(pl.BlockSpec((1, B), lambda i: (0, 0)), rows, rows),
    )(*parts)
    return loss.reshape(B), di, dt


def solution(mesh):
    return jax.shard_map(
        body,
        mesh=mesh,
        in_specs=(P(("img", "txt"), None), P(("img", "txt"), None), P(("img", "txt")), P(), P()),
        out_specs=(P(("img", "txt")), P(("img", "txt"), None), P(("img", "txt"), None)),
        check_vma=False,
    )
```
